256 devices in a mesh: img: 32 (over x, y, core), txt: 8 (over z).
Axes of the slice: x: 4, y: 4, z: 8, core: 2. Of those that a mesh axis runs over, the one named last changes fastest.
Arguments:
- image_emb: bfloat16 [16384, 1280], P(('img', 'txt')), may hold values from -100 to 100, as said below
- text_emb: bfloat16 [16384, 1280], P(('img', 'txt')), may hold values from -100 to 100, as said below
- log_scale: float32 [1], replicated, may hold values from 3 to 6
Outputs:
- loss: float32 [1], replicated
- grad_image: bfloat16 [16384, 1280], P(('img', 'txt'))
- grad_text: bfloat16 [16384, 1280], P(('img', 'txt'))
The draws below stay inside these ranges and needn't reach their ends.
Inputs may be any that keep to these rules, and one draw needn't show every extreme that they name: `image_emb`: each row is a direction times a row scale. `text_emb`: each row is a direction times a row scale.
All inputs are finite; a program needn't handle non-finite values.
Results may differ from the reference program's by a relative error of at most 0.011.
Values may be sent and summed in bfloat16 or wider, within the bound.
No kernel may reach another device: no remote copies, remote signals or barrier semaphores. Data moves between devices by JAX's collectives and lax.ppermute only.
A program may use at most 64 MiB of HBM per device.

```python
import math
import jax
import jax.numpy as jnp
from jax import lax

D = 1280
ROWS = 512
BATCH = 16384


def anchor_rows(key):
    return jax.random.normal(key, (BATCH, D), jnp.float32)


def row_scales(key, top):
    return jnp.exp(jax.random.uniform(key, (BATCH, 1), jnp.float32, 0.0, math.log(top)))


def pair_weight():
    index = jnp.arange(BATCH).astype(jnp.float32)
    return (0.9 * (1.0 - index / BATCH))[:, None]


def draw_image_emb(key, part):
    shared = anchor_rows(key)
    key = jax.random.fold_in(key, 11)
    own = jnp.clip(jax.random.normal(key, (BATCH, D), jnp.float32), -6.0, 6.0)
    mix = pair_weight()
    own = mix * shared + (1.0 - mix) * own
    values = own * row_scales(jax.random.fold_in(key, 1), 10.0)
    return jnp.clip(values, -100.0, 100.0).astype(jnp.bfloat16)


def draw_text_emb(key, part):
    shared = anchor_rows(key)
    key = jax.random.fold_in(key, 23)
    own = jnp.clip(jax.random.normal(key, (BATCH, D), jnp.float32), -6.0, 6.0)
    mix = pair_weight()
    own = mix * shared + (1.0 - mix) * own
    values = own * row_scales(jax.random.fold_in(key, 1), 10.0)
    return jnp.clip(values, -100.0, 100.0).astype(jnp.bfloat16)


def draw_log_scale(key, part):
    key = jax.random.fold_in(key, 37)
    return jax.random.uniform(key, (1,), jnp.float32, 3.0, 6.0)


def setup_inputs(seed: int = 0) -> dict:
    key_of = jax.random.split(jax.random.key(seed), 4)
    return {
        "image_emb": draw_image_emb(jax.random.fold_in(key_of[3], 71), 0),
        "text_emb": draw_text_emb(jax.random.fold_in(key_of[3], 71), 0),
        "log_scale": draw_log_scale(jax.random.fold_in(key_of[3], 71), 0),
    }


def unit_rows(raw):
    values = raw.astype(jnp.float32)
    norm = jnp.sqrt(lax.optimization_barrier(jnp.sum(values * values, axis=1)) + 1e-06)
    return (values / norm[:, None], norm)

def reference(image_emb, text_emb, log_scale):
    image_dir, image_norm = unit_rows(image_emb)
    text_dir, text_norm = unit_rows(text_emb)
    image_unit = image_dir.astype(jnp.bfloat16)
    text_unit = text_dir.astype(jnp.bfloat16)
    scale = jnp.exp(log_scale[0])
    blocks = image_unit.reshape(BATCH // ROWS, ROWS, D)
    starts = jnp.arange(BATCH // ROWS, dtype=jnp.int32) * ROWS
    columns = jnp.arange(BATCH, dtype=jnp.int32)
    dims = (((1,), (1,)), ((), ()))

    def first(carry, item):
        block, start = item
        top, total = carry
        logits = scale * lax.dot_general(block, text_unit, dims, preferred_element_type=jnp.float32)
        row_top = lax.optimization_barrier(jnp.max(logits, axis=1))
        row_lse = row_top + jnp.log(lax.optimization_barrier(jnp.sum(jnp.exp(logits - row_top[:, None]), axis=1)))
        rows = start + jnp.arange(ROWS, dtype=jnp.int32)
        mask = (rows[:, None] == columns[None, :]).astype(jnp.float32)
        diag = jnp.sum(logits * mask)
        newtop = jnp.maximum(top, lax.optimization_barrier(jnp.max(logits, axis=0)))
        total = total * jnp.exp(top - newtop) + lax.optimization_barrier(jnp.sum(jnp.exp(logits - newtop[None, :]), axis=0))
        return ((newtop, total), (row_lse, diag))
    init = (jnp.full((BATCH,), -1e+30, jnp.float32), jnp.zeros((BATCH,), jnp.float32))
    (col_top, col_total), (row_lse, diags) = lax.scan(first, init, (blocks, starts))
    col_lse = col_top + jnp.log(col_total)
    loss = (jnp.sum(row_lse) + jnp.sum(col_lse) - 2.0 * jnp.sum(diags)) / (2.0 * BATCH)

    def second(text_acc, item):
        block, start, block_lse = item
        logits = scale * lax.dot_general(block, text_unit, dims, preferred_element_type=jnp.float32)
        rows = start + jnp.arange(ROWS, dtype=jnp.int32)
        mask = (rows[:, None] == columns[None, :]).astype(jnp.float32)
        weights = ((jnp.exp(logits - block_lse[:, None]) + jnp.exp(logits - col_lse[None, :]) - 2.0 * mask) * 0.5).astype(jnp.bfloat16)
        image_back = scale * jnp.dot(weights, text_unit, preferred_element_type=jnp.float32)
        text_acc = text_acc + scale * lax.dot_general(weights, block, (((0,), (0,)), ((), ())), preferred_element_type=jnp.float32)
        return (text_acc, image_back)
    text_back, image_back = lax.scan(second, jnp.zeros((BATCH, D), jnp.float32), (blocks, starts, row_lse))
    image_back = image_back.reshape(BATCH, D)
    grad_image = (image_back - image_dir * lax.optimization_barrier(jnp.sum(image_dir * image_back, axis=1))[:, None]) / image_norm[:, None]
    grad_text = (text_back - text_dir * lax.optimization_barrier(jnp.sum(text_dir * text_back, axis=1))[:, None]) / text_norm[:, None]
    return (loss.reshape(1), grad_image.astype(jnp.bfloat16), grad_text.astype(jnp.bfloat16))
```

```python
import functools
import math

import jax
import jax.numpy as jnp
import numpy as np
from jax import lax
from jax.experimental import pallas as pl
from jax.experimental.pallas import tpu as pltpu
from jax.sharding import Mesh, PartitionSpec as P

LOG2E = math.log2(math.e)
LN2 = math.log(2.0)
EPS = 1e-06
VMEM = pltpu.CompilerParams(vmem_limit_bytes=40 * 1024 * 1024)
WHOLE = pl.BlockSpec(memory_space=pltpu.VMEM)
SCALAR = pl.BlockSpec(memory_space=pltpu.SMEM)
F32 = jnp.float32
BF16 = jnp.bfloat16


GRID = (4, 4, 2, 8)
INDEX = np.arange(256).reshape(GRID)
XY = INDEX.transpose(2, 3, 0, 1).reshape(16, 16).tolist()
CZ = INDEX.reshape(16, 16).tolist()
Z = INDEX.reshape(32, 8).tolist()
SWAP = [(int(a), int(b)) for c in (0, 1) for a, b in zip(INDEX[:, :, c].ravel(), INDEX[:, :, 1 - c].ravel())]
PEERS = 16
PIECE = 64
SIDE = PEERS * PIECE
TILE = 256
STEPS = SIDE // TILE


def unit_rows(raw):
    values = raw.astype(F32)
    norm = jnp.sqrt(jnp.sum(values * values, axis=1, keepdims=True) + EPS)
    return values / norm, norm


def image_unit_kernel(raw_ref, out_ref):
    out_ref[...] = unit_rows(raw_ref[...])[0].astype(BF16)


def text_unit_kernel(raw_ref, out_ref):
    unit = unit_rows(raw_ref[...])[0].astype(BF16)
    for k in range(PEERS):
        out_ref[pl.ds(k * PIECE, PIECE), :] = unit


def to_lanes(column):
    wide = jnp.broadcast_to(column, (column.shape[0], 128))
    return wide.T[:1, :]


def to_rows(lanes):
    wide = jnp.broadcast_to(lanes, (128, lanes.shape[1]))
    return wide.T[:, :1]


def logits_kernel(scale_ref, image_ref, text_ref, logits_ref, row_ref, col_ref, top_ref, sum_ref):
    step = pl.program_id(0)
    logits = lax.dot_general(
        image_ref[...], text_ref[...], (((1,), (1,)), ((), ())), preferred_element_type=F32
    ) * (scale_ref[0] * LOG2E)
    logits_ref[...] = logits
    row_top = jnp.max(logits, axis=1, keepdims=True)
    row_sum = jnp.sum(jnp.exp2(logits - row_top), axis=1, keepdims=True)
    row_lse = row_top + jnp.log2(row_sum)
    row_ref[...] = jnp.broadcast_to(to_lanes(row_lse), row_ref.shape)

    @pl.when(step == 0)
    def _():
        top_ref[...] = jnp.full_like(top_ref, -1e30)
        sum_ref[...] = jnp.zeros_like(sum_ref)

    top = jnp.maximum(top_ref[...], jnp.max(logits, axis=0, keepdims=True))
    sums = sum_ref[...] * jnp.exp2(top_ref[...] - top) + jnp.sum(
        jnp.exp2(logits - top), axis=0, keepdims=True
    )
    top_ref[...] = top
    sum_ref[...] = sums

    @pl.when(step == STEPS - 1)
    def _():
        col_ref[...] = jnp.broadcast_to(top + jnp.log2(sums), col_ref.shape)


def join_lse(parts):
    top = jnp.max(parts, axis=0, keepdims=True)
    return top + jnp.log2(jnp.sum(jnp.exp2(parts - top), axis=0, keepdims=True))


def row_tile(step, at_ref):
    return lax.rem(step + 2 * (1 - at_ref[2]), STEPS)


def weights_kernel(
    at_ref, scale_ref, logits_ref, text_ref, rows_ref, cols_ref,
    weights_ref, other_ref, mine_ref, loss_ref, part_ref,
):
    step = pl.program_id(0)
    tile = row_tile(step, at_ref)
    logits = logits_ref[...]
    row_lse = join_lse(rows_ref[...])
    col_lse = join_lse(cols_ref[...])
    row_at = lax.broadcasted_iota(jnp.int32, logits.shape, 0) + (tile * TILE - at_ref[0] * PIECE)
    col_at = lax.broadcasted_iota(jnp.int32, logits.shape, 1) - at_ref[1] * PIECE
    same = (row_at == col_at) & (row_at >= 0) & (row_at < PIECE)
    weights = (
        jnp.exp2(logits - to_rows(row_lse))
        + jnp.exp2(logits - col_lse)
        - jnp.where(same, 2.0, 0.0)
    ) * 0.5
    weights = weights.astype(BF16)
    weights_ref[...] = weights
    back = scale_ref[0] * jnp.dot(weights, text_ref[...], preferred_element_type=F32)

    @pl.when(step < STEPS // 2)
    def _():
        other_ref[...] = back.astype(BF16)

    @pl.when(step >= STEPS // 2)
    def _():
        mine_ref[...] = back

    @pl.when(step == 0)
    def _():
        part_ref[...] = jnp.sum(col_lse, axis=1, keepdims=True) * (1.0 / PEERS)

    part_ref[...] += (
        jnp.sum(row_lse, axis=1, keepdims=True) * (1.0 / PEERS)
        - 2.0 * jnp.sum(jnp.where(same, logits, 0.0), keepdims=True)
    )
    loss_ref[...] = jnp.broadcast_to(part_ref[...], loss_ref.shape)


def text_back_kernel(scale_ref, weights_ref, image_ref, out_ref):
    out_ref[...] = (
        scale_ref[0]
        * lax.dot_general(
            weights_ref[...], image_ref[...], (((0,), (0,)), ((), ())), preferred_element_type=F32
        )
    ).astype(BF16)


def project(back, raw):
    direction, norm = unit_rows(raw)
    along = jnp.sum(direction * back, axis=1, keepdims=True)
    return ((back - direction * along) / norm).astype(BF16)


def text_grad_kernel(parts_ref, raw_ref, out_ref):
    back = parts_ref[pl.ds(0, PIECE), :].astype(F32)
    for k in range(1, PEERS):
        back += parts_ref[pl.ds(k * PIECE, PIECE), :].astype(F32)
    out_ref[...] = project(back, raw_ref[...])


def image_grad_kernel(back_ref, raw_ref, out_ref):
    out_ref[...] = project(back_ref[...], raw_ref[...])


def on_vmem(kernel, shape, dtype, count):
    return pl.pallas_call(
        kernel,
        out_shape=jax.ShapeDtypeStruct(shape, dtype),
        in_specs=[WHOLE] * count,
        out_specs=WHOLE,
        compiler_params=VMEM,
    )


def exchange(x, groups):
    return lax.all_to_all(x, "d", 0, 0, axis_index_groups=groups, tiled=True)


def body(image_emb, text_emb, log_scale):
    width = image_emb.shape[1]
    scale = jnp.exp(log_scale)
    me = lax.axis_index("d")
    core = (me // 8) % 2
    at = jnp.stack([me % 16, me // 16, core]).astype(jnp.int32)

    image_unit = on_vmem(image_unit_kernel, image_emb.shape, BF16, 1)(image_emb)
    image = lax.all_gather(image_unit, "d", axis=0, tiled=True, axis_index_groups=CZ)
    text_units = on_vmem(text_unit_kernel, (SIDE, width), BF16, 1)(text_emb)
    text = exchange(text_units, XY)

    logits, row_part, col_part = pl.pallas_call(
        logits_kernel,
        grid=(STEPS,),
        in_specs=[
            SCALAR,
            pl.BlockSpec((TILE, width), lambda i: (i, 0)),
            pl.BlockSpec((SIDE, width), lambda i: (0, 0)),
        ],
        out_specs=[
            pl.BlockSpec((TILE, SIDE), lambda i: (i, 0)),
            pl.BlockSpec((PEERS, TILE), lambda i: (0, i)),
            pl.BlockSpec((PEERS, SIDE), lambda i: (0, 0)),
        ],
        out_shape=[
            jax.ShapeDtypeStruct((SIDE, SIDE), F32),
            jax.ShapeDtypeStruct((PEERS, SIDE), F32),
            jax.ShapeDtypeStruct((PEERS, SIDE), F32),
        ],
        scratch_shapes=[pltpu.VMEM((1, SIDE), F32), pltpu.VMEM((1, SIDE), F32)],
        compiler_params=VMEM,
    )(scale, image, text)

    rows = exchange(row_part, CZ)
    cols = exchange(col_part, XY)

    weights, other, mine, loss_part = pl.pallas_call(
        weights_kernel,
        grid_spec=pltpu.PrefetchScalarGridSpec(
            num_scalar_prefetch=1,
            grid=(STEPS,),
            in_specs=[
                SCALAR,
                pl.BlockSpec((TILE, SIDE), lambda i, at: (row_tile(i, at), 0)),
                pl.BlockSpec((SIDE, width), lambda i, at: (0, 0)),
                pl.BlockSpec((PEERS, TILE), lambda i, at: (0, row_tile(i, at))),
                pl.BlockSpec((PEERS, SIDE), lambda i, at: (0, 0)),
            ],
            out_specs=[
                pl.BlockSpec((TILE, SIDE), lambda i, at: (row_tile(i, at), 0)),
                pl.BlockSpec((TILE, width), lambda i, at: (jnp.minimum(i, STEPS // 2 - 1), 0)),
                pl.BlockSpec((TILE, width), lambda i, at: (jnp.maximum(i - STEPS // 2, 0), 0)),
                pl.BlockSpec((PEERS, 128), lambda i, at: (0, 0)),
            ],
            scratch_shapes=[pltpu.VMEM((1, 1), F32)],
        ),
        out_shape=[
            jax.ShapeDtypeStruct((SIDE, SIDE), BF16),
            jax.ShapeDtypeStruct((SIDE // 2, width), BF16),
            jax.ShapeDtypeStruct((SIDE // 2, width), F32),
            jax.ShapeDtypeStruct((PEERS, 128), F32),
        ],
        compiler_params=VMEM,
    )(at, scale, logits, text, rows, cols)

    swapped = lax.ppermute(other, "d", SWAP)
    text_parts = pl.pallas_call(
        text_back_kernel,
        grid=(STEPS,),
        in_specs=[
            SCALAR,
            pl.BlockSpec((SIDE, TILE), lambda j: (0, j)),
            pl.BlockSpec((SIDE, width), lambda j: (0, 0)),
        ],
        out_specs=pl.BlockSpec((TILE, width), lambda j: (j, 0)),
        out_shape=jax.ShapeDtypeStruct((SIDE, width), BF16),
        compiler_params=VMEM,
    )(scale, weights, image)
    image_sum = mine + swapped.astype(F32)
    image_back = lax.psum_scatter(
        image_sum, "d", scatter_dimension=0, axis_index_groups=Z, tiled=True
    )
    text_back = exchange(text_parts, XY)

    loss = exchange(loss_part, XY)
    loss = jnp.broadcast_to(jnp.sum(loss, axis=0, keepdims=True), loss.shape)
    loss = jnp.sum(exchange(loss, CZ), axis=0)[:1] * (LN2 / (2.0 * SIDE * PEERS))

    grad_image = on_vmem(image_grad_kernel, image_emb.shape, BF16, 2)(image_back, image_emb)
    grad_text = on_vmem(text_grad_kernel, text_emb.shape, BF16, 2)(text_back, text_emb)
    return loss, grad_image, grad_text


def solution(mesh):
    flat = Mesh(mesh.devices.reshape(-1), ("d",))
    return jax.shard_map(
        body,
        mesh=flat,
        in_specs=(P("d", None), P("d", None), P()),
        out_specs=(P(), P("d", None), P("d", None)),
        check_vma=False,
    )
```

```python
import functools
import math
import typing

import jax
import jax.numpy as jnp
import numpy as np
from jax import lax
from jax.experimental import pallas as pl
from jax.experimental.pallas import tpu as pltpu
from jax.sharding import Mesh, PartitionSpec as P

LOG2E = math.log2(math.e)
LN2 = math.log(2.0)
EPS = 1e-06
LOW = -1e30
PARAMS = pltpu.CompilerParams(vmem_limit_bytes=24 * 1024 * 1024)
HBM = pl.BlockSpec(memory_space=pl.ANY)
WHOLE = pl.BlockSpec(memory_space=pltpu.VMEM)
SCALAR = pl.BlockSpec(memory_space=pltpu.SMEM)
F32 = jnp.float32
BF16 = jnp.bfloat16

INDEX = np.arange(256).reshape(4, 4, 2, 8)
AXES = {"x": 0, "y": 1, "c": 2, "z": 3}
XY = INDEX.transpose(2, 3, 0, 1).reshape(16, 16).tolist()
MIXED = INDEX[:, :, 0, :].transpose(2, 0, 1).reshape(8, 16).tolist() + (
    INDEX[:, :, 1, :].reshape(2, 2, 4, 8).transpose(0, 2, 1, 3).reshape(8, 16).tolist()
)
PEERS = 16
PIECE = 64
SIDE = PEERS * PIECE
TILE = 256
STEPS = SIDE // TILE
DEEP = 8
LINES = 4 * STEPS


def shift(axis, by):
    to = np.roll(INDEX, -by, AXES[axis])
    return [(int(a), int(b)) for a, b in zip(INDEX.ravel(), to.ravel())]


def send(x, axis, by):
    return lax.ppermute(x, "d", shift(axis, by))


def exchange(x, groups):
    return lax.all_to_all(x, "d", 0, 0, axis_index_groups=groups, tiled=True)


def array(shape, dtype):
    return pltpu.HBM(shape, dtype)


def local(shape, dtype):
    return pltpu.VMEM(shape, dtype)


def call(kernel, outputs, *operands, scratch=(), aliases={}):
    specs, arrays = [], []
    for x in operands:
        if isinstance(x, Outside):
            specs.append(HBM)
            arrays.append(pltpu.with_memory_space_constraint(x.array, pltpu.HBM))
        elif x.size <= 8:
            specs.append(SCALAR)
            arrays.append(x)
        else:
            specs.append(WHOLE)
            arrays.append(pltpu.with_memory_space_constraint(x, pltpu.VMEM))
    return pl.pallas_call(
        kernel,
        out_shape=outputs,
        in_specs=specs,
        out_specs=jax.tree.map(lambda s: WHOLE if s.memory_space == pltpu.VMEM else HBM, outputs),
        scratch_shapes=list(scratch),
        input_output_aliases=aliases,
        compiler_params=PARAMS,
    )(*arrays)


class Outside(typing.NamedTuple):
    array: typing.Any


def run(copies):
    for copy in copies:
        copy.start()
    return copies


def wait(copies):
    for copy in copies:
        copy.wait()


def unit_rows(raw):
    values = raw.astype(F32)
    norm = jnp.sqrt(jnp.sum(values * values, axis=1, keepdims=True) + EPS)
    return values / norm, norm


def image_unit_kernel(raw_ref, out_ref, raw, unit, sem):
    wait(run([pltpu.make_async_copy(raw_ref, raw, sem.at[0])]))
    unit[...] = unit_rows(raw[...])[0].astype(BF16)
    wait(run([pltpu.make_async_copy(unit, out_ref, sem.at[0])]))


def text_units_kernel(raw_ref, out_ref, raw, unit, sem):
    wait(run([pltpu.make_async_copy(raw_ref, raw, sem.at[0])]))
    unit[...] = unit_rows(raw[...])[0].astype(BF16)
    wait(run([
        pltpu.make_async_copy(unit, out_ref.at[pl.ds(k * PIECE, PIECE), :], sem.at[k])
        for k in range(PEERS)
    ]))


def to_lanes(column):
    return jnp.broadcast_to(column, (column.shape[0], 128)).T[:1, :]


def to_rows(lanes):
    return jnp.broadcast_to(lanes, (128, lanes.shape[1])).T[:, :1]


def diagonal(at_ref):
    rows = pl.ds(pl.multiple_of(at_ref[0] * PIECE, PIECE), PIECE)
    cols = pl.ds(pl.multiple_of((at_ref[1] // 2) * 128, 128), 128)
    shape = (PIECE, 128)
    odd = lax.rem(at_ref[1], 2)
    at_row = lax.broadcasted_iota(jnp.int32, shape, 0) + odd * PIECE
    return rows, cols, at_row == lax.broadcasted_iota(jnp.int32, shape, 1)


def logits_kernel(plan, at_ref, scale_ref, text_ref, *refs):
    pieces = refs[: len(plan)]
    image_out, logits_ref, keep_ref, give_ref, image_ref, sem, out_sem = refs[len(plan) :]
    core = at_ref[2]
    copies = []
    for k, (piece, (flip, by, start, rows)) in enumerate(zip(pieces, plan)):
        block = lax.rem(core + flip, 2) * DEEP + lax.rem(at_ref[3] + by + DEEP, DEEP)
        first = pl.multiple_of(block * PIECE + start, 32)
        copies.append(pltpu.make_async_copy(piece, image_ref.at[pl.ds(first, rows), :], sem.at[k]))
    wait(run(copies))
    out = run([pltpu.make_async_copy(image_ref, image_out, out_sem.at[0])])
    text = text_ref[...]
    scale = scale_ref[0] * LOG2E
    top = jnp.full((1, SIDE), LOW, F32)
    sums = jnp.zeros((1, SIDE), F32)
    row_lse = []
    for k in range(STEPS):
        tile = slice(k * TILE, (k + 1) * TILE)
        logits = scale * lax.dot_general(
            image_ref[tile, :], text, (((1,), (1,)), ((), ())), preferred_element_type=F32
        )
        logits_ref[tile, :] = logits
        row_top = jnp.max(logits, axis=1, keepdims=True)
        row_sum = jnp.sum(jnp.exp2(logits - row_top), axis=1, keepdims=True)
        row_lse.append(to_lanes(row_top + jnp.log2(row_sum)))
        new = jnp.maximum(top, jnp.max(logits, axis=0, keepdims=True))
        sums = sums * jnp.exp2(top - new) + jnp.sum(jnp.exp2(logits - new), axis=0, keepdims=True)
        top = new
    col_lse = top + jnp.log2(sums)
    rows, cols, same = diagonal(at_ref)
    pairs = jnp.sum(jnp.where(same, logits_ref[rows, cols], 0.0), keepdims=True)
    first = core == 0
    for k in range(STEPS):
        part = col_lse[:, k * TILE : (k + 1) * TILE]
        keep_ref[k : k + 1, :] = jnp.where(first, part, row_lse[k])
        give_ref[k : k + 1, :] = jnp.where(first, row_lse[k], part)
    both = jnp.broadcast_to(pairs, (STEPS, TILE))
    keep_ref[STEPS:, :] = both
    give_ref[STEPS:, :] = both
    wait(out)


def spread_kernel(at_ref, keep_ref, recv_ref, out_ref):
    keep, recv = keep_ref[:STEPS, :], recv_ref[:STEPS, :]
    top = jnp.maximum(keep, recv)
    both = top + jnp.log2(jnp.exp2(keep - top) + jnp.exp2(recv - top))
    pairs = keep_ref[STEPS:, :] + recv_ref[STEPS:, :]
    first = at_ref[2] == 0
    block = jnp.concatenate(
        [jnp.where(first, keep, both), jnp.where(first, recv, both), pairs, pairs], axis=0
    )
    for k in range(PEERS):
        out_ref[pl.ds(k * LINES, LINES), :] = block


def join_kernel(at_ref, parts_ref, keep_ref, give_ref, loss_ref):
    parts = parts_ref[...].reshape(PEERS, LINES, TILE)
    pairs = jnp.sum(parts[:, 2 * STEPS : 2 * STEPS + 1, :1], axis=0)
    parts = parts[:, : 2 * STEPS, :]
    half = lax.broadcasted_iota(jnp.int32, parts.shape, 0) // DEEP
    first = at_ref[2] == 0
    parts = jnp.where(first | (half == at_ref[4]), parts, LOW)
    top = jnp.max(parts, axis=0)
    lse = top + jnp.log2(jnp.sum(jnp.exp2(parts - top[None]), axis=0))
    keep_ref[...] = lse[:STEPS]
    give_ref[...] = jnp.where(first, lse[STEPS:], lse[:STEPS])
    low = jnp.sum(lse[:STEPS], keepdims=True)
    high = jnp.sum(lse[STEPS:], keepdims=True)
    loss_ref[...] = jnp.broadcast_to(jnp.where(first, low + high - 2.0 * pairs, low), loss_ref.shape)


def weights_kernel(
    at_ref, scale_ref, logits_ref, text_ref, keep_ref, recv_ref,
    weights_ref, other_ref, mine_out, mine, sem,
):
    first = at_ref[2] == 0
    keep, recv = keep_ref[...], recv_ref[...]
    cols = jnp.where(first, keep, recv)
    col_lse = jnp.concatenate([cols[k : k + 1] for k in range(STEPS)], axis=1)
    rows = jnp.where(first, recv, keep)
    row_lse = [to_rows(rows[k : k + 1]) for k in range(STEPS)]
    for k in range(STEPS):
        tile = slice(k * TILE, (k + 1) * TILE)
        logits = logits_ref[tile, :]
        weights_ref[tile, :] = (
            (jnp.exp2(logits - row_lse[k]) + jnp.exp2(logits - col_lse)) * 0.5
        ).astype(BF16)

    own_rows, own_cols, same = diagonal(at_ref)
    logits = logits_ref[own_rows, own_cols]
    at_row = jnp.zeros((PIECE, 1), F32)
    for k in range(SIDE // PIECE):
        part = row_lse[k // STEPS][(k % STEPS) * PIECE : (k % STEPS + 1) * PIECE]
        at_row = jnp.where(at_ref[0] == k, part, at_row)
    at_col = jnp.zeros((1, 128), F32)
    for k in range(SIDE // 128):
        at_col = jnp.where(at_ref[1] // 2 == k, col_lse[:, k * 128 : (k + 1) * 128], at_col)
    weights_ref[own_rows, own_cols] = (
        (jnp.exp2(logits - at_row) + jnp.exp2(logits - at_col) - jnp.where(same, 2.0, 0.0)) * 0.5
    ).astype(BF16)

    text = text_ref[...]
    for k in range(STEPS // 2):
        tile = slice(k * TILE, (k + 1) * TILE)
        theirs = pl.ds(pl.multiple_of((1 - at_ref[2]) * (SIDE // 2) + k * TILE, TILE), TILE)
        other_ref[tile, :] = (
            scale_ref[0] * jnp.dot(weights_ref[theirs, :], text, preferred_element_type=F32)
        ).astype(BF16)


    copies = []
    for k in range(STEPS // 2):
        tile = slice(k * TILE, (k + 1) * TILE)
        ours = pl.ds(pl.multiple_of(at_ref[2] * (SIDE // 2) + k * TILE, TILE), TILE)
        mine[tile, :] = scale_ref[0] * jnp.dot(weights_ref[ours, :], text, preferred_element_type=F32)
        copies += run([pltpu.make_async_copy(mine.at[tile, :], mine_out.at[tile, :], sem.at[k])])
    wait(copies)


def back_tile(k, scale_ref, weights_ref, image, back, out_ref, sem):
    tile = slice(k * TILE, (k + 1) * TILE)
    back[tile, :] = (
        scale_ref[0]
        * lax.dot_general(
            weights_ref[:, tile], image, (((0,), (0,)), ((), ())), preferred_element_type=F32
        )
    ).astype(BF16)
    return run([pltpu.make_async_copy(back.at[tile, :], out_ref.at[tile, :], sem.at[k])])


def text_back_kernel(scale_ref, weights_ref, image_ref, out_ref, back, sem):
    image = image_ref[...]
    copies = []
    for k in range(STEPS - 1):
        copies += back_tile(k, scale_ref, weights_ref, image, back, out_ref, sem)
    wait(copies)


def pieces_kernel(at_ref, scale_ref, weights_ref, image_ref, swapped_ref, mine_ref, begun_ref, *refs):
    out_ref, own_ref, *out_refs, mine, back, sem = refs
    loads = run([pltpu.make_async_copy(mine_ref, mine, sem.at[0])])
    copies = back_tile(STEPS - 1, scale_ref, weights_ref, image_ref[...], back, out_ref, sem)
    wait(loads)
    for k in range(DEEP):
        block = pl.ds(pl.multiple_of(lax.rem(at_ref[3] + k, DEEP) * PIECE, PIECE), PIECE)
        total = mine[block, :] + swapped_ref[block, :].astype(F32)
        if k == 0:
            own_ref[...] = total
        else:
            out_refs[k - 1][...] = total.astype(BF16)
    wait(copies)


def project(back, raw):
    direction, norm = unit_rows(raw)
    along = jnp.sum(direction * back, axis=1, keepdims=True)
    return ((back - direction * along) / norm).astype(BF16)


def text_grad_kernel(raw_ref, parts_ref, out_ref, raw, grad, sem):
    wait(run([pltpu.make_async_copy(raw_ref, raw, sem.at[0])]))
    back = parts_ref[pl.ds(0, PIECE), :].astype(F32)
    for k in range(1, PEERS):
        back += parts_ref[pl.ds(k * PIECE, PIECE), :].astype(F32)
    grad[...] = project(back, raw[...])
    wait(run([pltpu.make_async_copy(grad, out_ref, sem.at[0])]))


def image_grad_kernel(raw_ref, own_ref, part_ref, *refs):
    pieces, (out_ref, loss_ref, raw, grad, sem) = refs[:-5], refs[-5:]
    loss_ref[...] = part_ref[...]
    wait(run([pltpu.make_async_copy(raw_ref, raw, sem.at[0])]))
    back = own_ref[...]
    for ref in pieces:
        back += ref[...].astype(F32)
    grad[...] = project(back, raw[...])
    wait(run([pltpu.make_async_copy(grad, out_ref, sem.at[0])]))


def gather_image(unit):
    plan, arrays = [(0, 0, 0, PIECE)], [unit]
    up, down, half = unit, unit, PIECE // 2
    for by in range(1, DEEP // 2):
        up, down = send(up, "z", 1), send(down, "z", -1)
        plan += [(0, -by, 0, PIECE), (0, by, 0, PIECE)]
        arrays += [up, down]
    plan += [(0, -(DEEP // 2), 0, half), (0, DEEP // 2, half, half)]
    arrays += [send(up[:half], "z", 1), send(down[half:], "z", -1)]
    plan += [(1, *rest) for _, *rest in plan]
    arrays += [send(a, "c", 1) for a in arrays]
    return plan, arrays


def sum_step(part, first, second):
    held = []
    for k in range(3):
        pairs = [(a, b) for a, b in shift(second, k + 1) if a // 8 % 2 == 1]
        if k < len(first):
            pairs += [(a, b) for a, b in shift("z", first[k]) if a // 8 % 2 == 0]
        held.append(lax.ppermute(part, "d", pairs))
    return (part + held[1]) + (held[0] + held[2])


def body(image_emb, text_emb, log_scale):
    width = image_emb.shape[1]
    scale = jnp.exp(log_scale)
    me = lax.axis_index("d")
    z, core, x = me % 8, (me // 8) % 2, me // 64
    at = jnp.stack([me % 16, me // 16, core, z, x % 2]).astype(jnp.int32)
    piece = local((PIECE, width), BF16)
    side = local((SIDE, width), BF16)
    outside = array((SIDE, width), BF16)
    raw = pltpu.VMEM((PIECE, width), BF16)
    sems = pltpu.SemaphoreType.DMA

    image_unit = call(image_unit_kernel, array((PIECE, width), BF16), Outside(image_emb), scratch=[raw, raw, sems((1,))])
    plan, pieces = gather_image(image_unit)
    text_units = call(text_units_kernel, outside, Outside(text_emb), scratch=[raw, raw, sems((PEERS,))])
    text = exchange(text_units, XY)

    lines = local((2 * STEPS, TILE), F32)
    image, logits, keep, give = call(
        functools.partial(logits_kernel, plan), [outside, local((SIDE, SIDE), F32), lines, lines],
        at, scale, text, *map(Outside, pieces),
        scratch=[pltpu.VMEM((SIDE, width), BF16), sems((len(plan),)), sems((1,))],
    )
    spread = call(spread_kernel, local((PEERS * LINES, TILE), F32), at, keep, send(give, "c", 1))
    lines = local((STEPS, TILE), F32)
    keep, give, part = call(join_kernel, [lines, lines, local((8, 128), F32)], at, exchange(spread, MIXED))
    recv = send(give, "c", 1)

    half = pltpu.VMEM((SIDE // 2, width), F32)
    weights, other, mine = call(
        weights_kernel,
        [local((SIDE, SIDE), BF16), local((SIDE // 2, width), BF16), array((SIDE // 2, width), F32)],
        at, scale, logits, text, keep, recv,
        scratch=[half, sems((STEPS // 2,))],
    )
    swapped = send(other, "c", 1)
    back = [pltpu.VMEM((SIDE, width), BF16), sems((STEPS,))]
    text_parts = call(text_back_kernel, outside, scale, weights, image, scratch=back)
    text_parts, own, *away = call(
        pieces_kernel, [outside, local((PIECE, width), F32)] + [piece] * (DEEP - 1),
        at, scale, weights, image, swapped, Outside(mine), Outside(text_parts),
        scratch=[half, *back], aliases={6: 0},
    )
    text_back = exchange(text_parts, XY)
    image_back = [send(a, "z", k + 1) for k, a in enumerate(away)]

    grad = array((PIECE, width), BF16)
    extra = [raw, raw, sems((1,))]
    grad_image, part = call(
        image_grad_kernel, [grad, local((8, 128), F32)], Outside(image_emb), own, part, *image_back, scratch=extra
    )
    part = sum_step(sum_step(part, (2, 4, 6), "x"), (1,), "y")
    loss = (part + send(part, "c", 1))[0, :1] * (LN2 / (2.0 * SIDE * PEERS))
    grad_text = call(text_grad_kernel, grad, Outside(text_emb), text_back, scratch=extra)
    return loss, grad_image, grad_text


def solution(mesh):
    flat = Mesh(mesh.devices.reshape(-1), ("d",))
    return jax.shard_map(
        body,
        mesh=flat,
        in_specs=(P("d", None), P("d", None), P()),
        out_specs=(P(), P("d", None), P("d", None)),
        check_vma=False,
    )
```

```python
import functools
import math
import typing

import jax
import jax.numpy as jnp
import numpy as np
from jax import lax
from jax.experimental import pallas as pl
from jax.experimental.pallas import tpu as pltpu
from jax.sharding import Mesh, PartitionSpec as P

LOG2E = math.log2(math.e)
LN2 = math.log(2.0)
EPS = 1e-06
LOW = -1e30
PARAMS = pltpu.CompilerParams(vmem_limit_bytes=24 * 1024 * 1024)
HBM = pl.BlockSpec(memory_space=pl.ANY)
WHOLE = pl.BlockSpec(memory_space=pltpu.VMEM)
SCALAR = pl.BlockSpec(memory_space=pltpu.SMEM)
F32 = jnp.float32
BF16 = jnp.bfloat16

INDEX = np.arange(256).reshape(4, 4, 2, 8)
AXES = {"x": 0, "y": 1, "c": 2, "z": 3}
XY = INDEX.transpose(2, 3, 0, 1).reshape(16, 16).tolist()
MIXED = INDEX[:, :, 0, :].transpose(2, 0, 1).reshape(8, 16).tolist() + (
    INDEX[:, :, 1, :].reshape(2, 2, 4, 8).transpose(0, 2, 1, 3).reshape(8, 16).tolist()
)
PEERS = 16
PIECE = 64
SIDE = PEERS * PIECE
TILE = 256
STEPS = SIDE // TILE
DEEP = 8
LINES = 4 * STEPS
WIDTH = 1280
WIDER = WIDTH + 128


def shift(axis, by):
    to = np.roll(INDEX, -by, AXES[axis])
    return [(int(a), int(b)) for a, b in zip(INDEX.ravel(), to.ravel())]


def send(x, axis, by):
    return lax.ppermute(x, "d", shift(axis, by))


def exchange(x, groups):
    return lax.all_to_all(x, "d", 0, 0, axis_index_groups=groups, tiled=True)


def array(shape, dtype):
    return pltpu.HBM(shape, dtype)


def local(shape, dtype):
    return pltpu.VMEM(shape, dtype)


def call(kernel, outputs, *operands, scratch=(), aliases={}):
    specs, arrays = [], []
    for x in operands:
        if isinstance(x, Outside):
            specs.append(HBM)
            arrays.append(pltpu.with_memory_space_constraint(x.array, pltpu.HBM))
        elif x.size <= 8:
            specs.append(SCALAR)
            arrays.append(x)
        else:
            specs.append(WHOLE)
            arrays.append(pltpu.with_memory_space_constraint(x, pltpu.VMEM))
    return pl.pallas_call(
        kernel,
        out_shape=outputs,
        in_specs=specs,
        out_specs=jax.tree.map(lambda s: {pltpu.VMEM: WHOLE, pltpu.SMEM: SCALAR}.get(s.memory_space, HBM), outputs),
        scratch_shapes=list(scratch),
        input_output_aliases=aliases,
        compiler_params=PARAMS,
    )(*arrays)


class Outside(typing.NamedTuple):
    array: typing.Any


def run(copies):
    for copy in copies:
        copy.start()
    return copies


def wait(copies):
    for copy in copies:
        copy.wait()


def unit_rows(raw):
    values = raw.astype(F32)
    norm = jnp.sqrt(jnp.sum(values * values, axis=1, keepdims=True) + EPS)
    return values / norm, norm


def image_unit_kernel(raw_ref, out_ref, raw, unit, sem):
    wait(run([pltpu.make_async_copy(raw_ref, raw, sem.at[0])]))
    unit[...] = unit_rows(raw[...])[0].astype(BF16)
    wait(run([pltpu.make_async_copy(unit, out_ref, sem.at[0])]))


def text_units_kernel(raw_ref, out_ref, raw, unit, sem):
    wait(run([pltpu.make_async_copy(raw_ref, raw, sem.at[0])]))
    unit[...] = unit_rows(raw[...])[0].astype(BF16)
    wait(run([
        pltpu.make_async_copy(unit, out_ref.at[pl.ds(k * PIECE, PIECE), :], sem.at[k])
        for k in range(PEERS)
    ]))


def to_lanes(column):
    return jnp.broadcast_to(column, (column.shape[0], 128)).T[:1, :]


def to_rows(lanes):
    return jnp.broadcast_to(lanes, (128, lanes.shape[1])).T[:, :1]


def diagonal(at_ref):
    rows = pl.ds(pl.multiple_of(at_ref[0] * PIECE, PIECE), PIECE)
    cols = pl.ds(pl.multiple_of((at_ref[1] // 2) * 128, 128), 128)
    shape = (PIECE, 128)
    odd = lax.rem(at_ref[1], 2)
    at_row = lax.broadcasted_iota(jnp.int32, shape, 0) + odd * PIECE
    return rows, cols, at_row == lax.broadcasted_iota(jnp.int32, shape, 1)


def logits_kernel(plan, at_ref, scale_ref, text_ref, *refs):
    pieces = refs[: len(plan)]
    image_out, logits_ref, keep_ref, give_ref, image_ref, sem, out_sem = refs[len(plan) :]
    core = at_ref[2]
    copies = []
    for k, (piece, (flip, by, start, rows)) in enumerate(zip(pieces, plan)):
        block = lax.rem(core + flip, 2) * DEEP + lax.rem(at_ref[3] + by + DEEP, DEEP)
        first = pl.multiple_of(block * PIECE + start, 32)
        copies.append(pltpu.make_async_copy(piece, image_ref.at[pl.ds(first, rows), :], sem.at[k]))
    run(copies)
    near = len(plan) // 2
    wait(copies[:near])
    text = text_ref[...]
    scale = scale_ref[0] * LOG2E
    top = jnp.full((1, SIDE), LOW, F32)
    sums = jnp.zeros((1, SIDE), F32)
    row_lse = []
    for k in range(STEPS):
        if k == STEPS // 2:
            wait(copies[near:])
            out = run([pltpu.make_async_copy(image_ref, image_out, out_sem.at[0])])
        tile = pl.ds(pl.multiple_of(lax.rem(core * 2 + k, STEPS) * TILE, TILE), TILE)
        logits = scale * lax.dot_general(
            image_ref[tile, :], text, (((1,), (1,)), ((), ())), preferred_element_type=F32
        )
        logits_ref[tile, :] = logits
        row_top = jnp.max(logits, axis=1, keepdims=True)
        row_sum = jnp.sum(jnp.exp2(logits - row_top), axis=1, keepdims=True)
        row_lse.append(to_lanes(row_top + jnp.log2(row_sum)))
        new = jnp.maximum(top, jnp.max(logits, axis=0, keepdims=True))
        sums = sums * jnp.exp2(top - new) + jnp.sum(jnp.exp2(logits - new), axis=0, keepdims=True)
        top = new
    col_lse = top + jnp.log2(sums)
    rows, cols, same = diagonal(at_ref)
    pairs = jnp.sum(jnp.where(same, logits_ref[rows, cols], 0.0), keepdims=True)
    first = core == 0
    row_lse = [jnp.where(first, row_lse[k], row_lse[(k + 2) % STEPS]) for k in range(STEPS)]
    for k in range(STEPS):
        part = col_lse[:, k * TILE : (k + 1) * TILE]
        keep_ref[k : k + 1, :] = jnp.where(first, part, row_lse[k])
        give_ref[k : k + 1, :] = jnp.where(first, row_lse[k], part)
    both = jnp.broadcast_to(pairs, (STEPS, TILE))
    keep_ref[STEPS:, :] = both
    give_ref[STEPS:, :] = both
    wait(out)


def spread_kernel(at_ref, keep_ref, recv_ref, out_ref):
    keep, recv = keep_ref[:STEPS, :], recv_ref[:STEPS, :]
    top = jnp.maximum(keep, recv)
    both = top + jnp.log2(jnp.exp2(keep - top) + jnp.exp2(recv - top))
    pairs = keep_ref[STEPS:, :] + recv_ref[STEPS:, :]
    first = at_ref[2] == 0
    block = jnp.concatenate(
        [jnp.where(first, keep, both), jnp.where(first, recv, both), pairs, pairs], axis=0
    )
    for k in range(PEERS):
        out_ref[pl.ds(k * LINES, LINES), :] = block


def join_kernel(at_ref, parts_ref, keep_ref, give_ref):
    parts = parts_ref[...].reshape(PEERS, LINES, TILE)
    pairs = jnp.sum(parts[:, 2 * STEPS : 2 * STEPS + 1, :1], axis=0)
    parts = parts[:, : 2 * STEPS, :]
    half = lax.broadcasted_iota(jnp.int32, parts.shape, 0) // DEEP
    first = at_ref[2] == 0
    parts = jnp.where(first | (half == at_ref[4]), parts, LOW)
    top = jnp.max(parts, axis=0)
    lse = top + jnp.log2(jnp.sum(jnp.exp2(parts - top[None]), axis=0))
    columns = jnp.broadcast_to(jnp.sum(lse, keepdims=True) - 2.0 * pairs, (STEPS, TILE))
    keep_ref[:STEPS, :] = lse[:STEPS]
    keep_ref[STEPS:, :] = columns
    give_ref[:STEPS, :] = jnp.where(first, lse[STEPS:], lse[:STEPS])
    give_ref[STEPS:, :] = columns


def tag(term):
    term = jnp.broadcast_to(term, (PIECE, 128))
    high = term.astype(BF16)
    rest = term - high.astype(F32)
    middle = rest.astype(BF16)
    low = (rest - middle.astype(F32)).astype(BF16)
    row = lax.broadcasted_iota(jnp.int32, (PIECE, 128), 0)
    return jnp.where(
        row < 16, high.astype(F32), jnp.where(row < 32, middle.astype(F32), low.astype(F32))
    ).astype(BF16)


def untag(block):
    block = block.astype(F32)
    return (block[0:1, :1] + block[16:17, :1]) + block[32:33, :1]


def weights_kernel(
    at_ref, scale_ref, logits_ref, text_ref, keep_ref, recv_ref,
    weights_ref, other_ref, sums_ref, mine_out, mine, sem,
):
    first = at_ref[2] == 0
    keep, recv = keep_ref[:STEPS, :], recv_ref[:STEPS, :]
    cols = jnp.where(first, keep, recv)
    col_lse = jnp.concatenate([cols[k : k + 1] for k in range(STEPS)], axis=1)
    rows = jnp.where(first, recv, keep)
    sums_ref[:STEPS, :] = jnp.broadcast_to(jnp.sum(rows, keepdims=True), (STEPS, 128))
    sums_ref[STEPS:, :] = jnp.where(first, keep_ref[STEPS:, :128], recv_ref[STEPS:, :128])
    row_lse = [to_rows(rows[k : k + 1]) for k in range(STEPS)]
    for k in range(STEPS):
        tile = slice(k * TILE, (k + 1) * TILE)
        logits = logits_ref[tile, :]
        weights_ref[tile, :] = (
            (jnp.exp2(logits - row_lse[k]) + jnp.exp2(logits - col_lse)) * 0.5
        ).astype(BF16)

    own_rows, own_cols, same = diagonal(at_ref)
    logits = logits_ref[own_rows, own_cols]
    at_row = jnp.zeros((PIECE, 1), F32)
    for k in range(SIDE // PIECE):
        part = row_lse[k // STEPS][(k % STEPS) * PIECE : (k % STEPS + 1) * PIECE]
        at_row = jnp.where(at_ref[0] == k, part, at_row)
    at_col = jnp.zeros((1, 128), F32)
    for k in range(SIDE // 128):
        at_col = jnp.where(at_ref[1] // 2 == k, col_lse[:, k * 128 : (k + 1) * 128], at_col)
    weights_ref[own_rows, own_cols] = (
        (jnp.exp2(logits - at_row) + jnp.exp2(logits - at_col) - jnp.where(same, 2.0, 0.0)) * 0.5
    ).astype(BF16)

    text = text_ref[...]
    for k in range(STEPS // 2):
        tile = slice(k * TILE, (k + 1) * TILE)
        theirs = pl.ds(pl.multiple_of((1 - at_ref[2]) * (SIDE // 2) + k * TILE, TILE), TILE)
        other_ref[tile, :] = (
            scale_ref[0] * jnp.dot(weights_ref[theirs, :], text, preferred_element_type=F32)
        ).astype(BF16)


    copies = []
    for k in range(STEPS // 2):
        tile = slice(k * TILE, (k + 1) * TILE)
        ours = pl.ds(pl.multiple_of(at_ref[2] * (SIDE // 2) + k * TILE, TILE), TILE)
        mine[tile, :] = scale_ref[0] * jnp.dot(weights_ref[ours, :], text, preferred_element_type=F32)
        copies += run([pltpu.make_async_copy(mine.at[tile, :], mine_out.at[tile, :], sem.at[k])])
    wait(copies)


def back_tile(k, scale_ref, weights_ref, image, mark, back, out_ref, sem):
    tile = slice(k * TILE, (k + 1) * TILE)
    back[tile, :WIDTH] = (
        scale_ref[0]
        * lax.dot_general(
            weights_ref[:, tile], image, (((0,), (0,)), ((), ())), preferred_element_type=F32
        )
    ).astype(BF16)
    back[tile, WIDTH:] = jnp.concatenate([mark] * (TILE // PIECE), axis=0)
    return run([pltpu.make_async_copy(back.at[tile, :], out_ref.at[tile, :], sem.at[k])])


def text_back_kernel(scale_ref, weights_ref, image_ref, sums_ref, out_ref, back, sem):
    image = image_ref[...]
    mark = tag(sums_ref[:1, :1])
    copies = []
    for k in range(STEPS - 1):
        copies += back_tile(k, scale_ref, weights_ref, image, mark, back, out_ref, sem)
    wait(copies)


def pieces_kernel(
    at_ref, scale_ref, weights_ref, image_ref, sums_ref, swapped_ref, mine_ref, begun_ref, *refs
):
    out_ref, own_ref, *out_refs, mine, parts, back, mine_sem, sem, back_sem = refs
    loads = run([pltpu.make_async_copy(mine_ref, mine, mine_sem.at[0])])
    copies = back_tile(
        STEPS - 1, scale_ref, weights_ref, image_ref[...], tag(sums_ref[:1, :1]), back, out_ref, back_sem
    )
    mark = tag(sums_ref[STEPS : STEPS + 1, :1])
    wait(loads)
    for k in range(DEEP):
        block = pl.ds(pl.multiple_of(lax.rem(at_ref[3] + k, DEEP) * PIECE, PIECE), PIECE)
        total = mine[block, :] + swapped_ref[block, :].astype(F32)
        if k == 0:
            own_ref[...] = total
        else:
            parts[k - 1, :, :WIDTH] = total.astype(BF16)
            parts[k - 1, :, WIDTH:] = mark
            copies += run([pltpu.make_async_copy(parts.at[k - 1], out_refs[k - 1], sem.at[k - 1])])
    wait(copies)


def project(back, raw):
    direction, norm = unit_rows(raw)
    along = jnp.sum(direction * back, axis=1, keepdims=True)
    return ((back - direction * along) / norm).astype(BF16)


def text_grad_kernel(raw_ref, loss_ref, parts_ref, out_ref, total_ref, raw, grad, sem):
    copies = run([pltpu.make_async_copy(raw_ref, raw, sem.at[0])])
    back = jnp.zeros((PIECE, WIDTH), F32)
    total = loss_ref[:1, :1]
    for k in range(PEERS):
        block = pl.ds(k * PIECE, PIECE)
        back += parts_ref[block, :WIDTH].astype(F32)
        total += untag(parts_ref[block, WIDTH:])
    total_ref[0] = (total * (LN2 / (2.0 * SIDE * PEERS)))[0, 0]
    wait(copies)
    grad[...] = project(back, raw[...])
    wait(run([pltpu.make_async_copy(grad, out_ref, sem.at[0])]))


def image_grad_kernel(raw_ref, own_ref, sums_ref, *refs):
    pieces, (out_ref, loss_ref, raw, grad, sem) = refs[:-5], refs[-5:]
    copies = run([pltpu.make_async_copy(raw_ref, raw, sem.at[0])])
    back = own_ref[...]
    held = [sums_ref[STEPS : STEPS + 1, :1]]
    for ref in pieces:
        back += ref[:, :WIDTH].astype(F32)
        held.append(untag(ref[:, WIDTH:]))
    while len(held) > 1:
        half = len(held) // 2
        held = [held[k] + held[k + half] for k in range(half)]
    loss_ref[...] = jnp.broadcast_to(held[0], loss_ref.shape)
    wait(copies)
    grad[...] = project(back, raw[...])
    wait(run([pltpu.make_async_copy(grad, out_ref, sem.at[0])]))


def gather_image(unit):
    plan, arrays = [(0, 0, 0, PIECE)], [unit]
    up, down, half = unit, unit, PIECE // 2
    for by in range(1, DEEP // 2):
        up, down = send(up, "z", 1), send(down, "z", -1)
        plan += [(0, -by, 0, PIECE), (0, by, 0, PIECE)]
        arrays += [up, down]
    plan += [(0, -(DEEP // 2), 0, half), (0, DEEP // 2, half, half)]
    arrays += [send(up[:half], "z", 1), send(down[half:], "z", -1)]
    plan += [(1, *rest) for _, *rest in plan]
    arrays += [send(a, "c", 1) for a in arrays]
    return plan, arrays


def body(image_emb, text_emb, log_scale):
    width = image_emb.shape[1]
    scale = jnp.exp(log_scale)
    me = lax.axis_index("d")
    z, core, x = me % 8, (me // 8) % 2, me // 64
    at = jnp.stack([me % 16, me // 16, core, z, x % 2]).astype(jnp.int32)
    piece = local((PIECE, width), BF16)
    side = local((SIDE, width), BF16)
    outside = array((SIDE, width), BF16)
    raw = pltpu.VMEM((PIECE, width), BF16)
    sems = pltpu.SemaphoreType.DMA

    image_unit = call(image_unit_kernel, array((PIECE, width), BF16), Outside(image_emb), scratch=[raw, raw, sems((1,))])
    plan, pieces = gather_image(image_unit)
    text_units = call(text_units_kernel, outside, Outside(text_emb), scratch=[raw, raw, sems((PEERS,))])
    text = exchange(text_units, XY)

    lines = local((2 * STEPS, TILE), F32)
    image, logits, keep, give = call(
        functools.partial(logits_kernel, plan), [outside, local((SIDE, SIDE), F32), lines, lines],
        at, scale, text, *map(Outside, pieces),
        scratch=[pltpu.VMEM((SIDE, width), BF16), sems((len(plan),)), sems((1,))],
    )
    spread = call(spread_kernel, local((PEERS * LINES, TILE), F32), at, keep, send(give, "c", 1))
    keep, give = call(join_kernel, [lines, lines], at, exchange(spread, MIXED))
    recv = send(give, "c", 1)

    half = pltpu.VMEM((SIDE // 2, width), F32)
    weights, other, sums, mine = call(
        weights_kernel,
        [
            local((SIDE, SIDE), BF16),
            local((SIDE // 2, width), BF16),
            local((2 * STEPS, 128), F32),
            array((SIDE // 2, width), F32),
        ],
        at, scale, logits, text, keep, recv,
        scratch=[half, sems((STEPS // 2,))],
    )
    swapped = send(other, "c", 1)
    back = pltpu.VMEM((SIDE, WIDER), BF16)
    wide = array((SIDE, WIDER), BF16)
    text_parts = call(
        text_back_kernel, wide, scale, weights, image, sums, scratch=[back, sems((STEPS,))]
    )
    text_parts, own, *away = call(
        pieces_kernel,
        [wide, local((PIECE, width), F32)] + [array((PIECE, WIDER), BF16)] * (DEEP - 1),
        at, scale, weights, image, sums, swapped, Outside(mine), Outside(text_parts),
        scratch=[
            half, pltpu.VMEM((DEEP - 1, PIECE, WIDER), BF16), back, sems((1,)), sems((DEEP - 1,)), sems((STEPS,))
        ],
        aliases={7: 0},
    )
    text_back = exchange(text_parts, XY)
    image_back = [send(a, "z", k + 1) for k, a in enumerate(away)]

    grad = array((PIECE, width), BF16)
    extra = [raw, raw, sems((1,))]
    grad_image, part = call(
        image_grad_kernel, [grad, local((8, 128), F32)], Outside(image_emb), own, sums, *image_back, scratch=extra
    )
    grad_text, loss = call(
        text_grad_kernel, [grad, pltpu.SMEM((1,), F32)], Outside(text_emb), part, text_back, scratch=extra
    )
    return loss, grad_image, grad_text


def solution(mesh):
    flat = Mesh(mesh.devices.reshape(-1), ("d",))
    return jax.shard_map(
        body,
        mesh=flat,
        in_specs=(P("d", None), P("d", None), P()),
        out_specs=(P(), P("d", None), P("d", None)),
        check_vma=False,
    )
```

```python
import functools
import math
import typing

import jax
import jax.numpy as jnp
import numpy as np
from jax import lax
from jax.experimental import pallas as pl
from jax.experimental.pallas import tpu as pltpu
from jax.sharding import Mesh, PartitionSpec as P

LOG2E = math.log2(math.e)
LN2 = math.log(2.0)
EPS = 1e-06
LOW = -1e30
PARAMS = pltpu.CompilerParams(vmem_limit_bytes=24 * 1024 * 1024)
HBM = pl.BlockSpec(memory_space=pl.ANY)
WHOLE = pl.BlockSpec(memory_space=pltpu.VMEM)
SCALAR = pl.BlockSpec(memory_space=pltpu.SMEM)
F32 = jnp.float32
BF16 = jnp.bfloat16

INDEX = np.arange(256).reshape(4, 4, 2, 8)
AXES = {"x": 0, "y": 1, "c": 2, "z": 3}
XY = INDEX.transpose(2, 3, 0, 1).reshape(16, 16).tolist()
MIXED = INDEX[:, :, 0, :].transpose(2, 0, 1).reshape(8, 16).tolist() + (
    INDEX[:, :, 1, :].reshape(2, 2, 4, 8).transpose(0, 2, 1, 3).reshape(8, 16).tolist()
)
PEERS = 16
PIECE = 64
SIDE = PEERS * PIECE
TILE = 256
STEPS = SIDE // TILE
DEEP = 8
LINES = 4 * STEPS
WIDTH = 1280
WIDER = WIDTH + 128
MARK = 16
PART = PIECE * (WIDTH // 128) + MARK


def shift(axis, by):
    to = np.roll(INDEX, -by, AXES[axis])
    return [(int(a), int(b)) for a, b in zip(INDEX.ravel(), to.ravel())]


def send(x, axis, by):
    return lax.ppermute(x, "d", shift(axis, by))


def exchange(x, groups):
    return lax.all_to_all(x, "d", 0, 0, axis_index_groups=groups, tiled=True)


def array(shape, dtype):
    return pltpu.HBM(shape, dtype)


def local(shape, dtype):
    return pltpu.VMEM(shape, dtype)


def call(kernel, outputs, *operands, scratch=(), aliases={}):
    specs, arrays = [], []
    for x in operands:
        if isinstance(x, Outside):
            specs.append(HBM)
            arrays.append(pltpu.with_memory_space_constraint(x.array, pltpu.HBM))
        elif x.size <= 8:
            specs.append(SCALAR)
            arrays.append(x)
        else:
            specs.append(WHOLE)
            arrays.append(pltpu.with_memory_space_constraint(x, pltpu.VMEM))
    return pl.pallas_call(
        kernel,
        out_shape=outputs,
        in_specs=specs,
        out_specs=jax.tree.map(lambda s: {pltpu.VMEM: WHOLE, pltpu.SMEM: SCALAR}.get(s.memory_space, HBM), outputs),
        scratch_shapes=list(scratch),
        input_output_aliases=aliases,
        compiler_params=PARAMS,
    )(*arrays)


class Outside(typing.NamedTuple):
    array: typing.Any


def run(copies):
    for copy in copies:
        copy.start()
    return copies


def wait(copies):
    for copy in copies:
        copy.wait()


def unit_rows(raw):
    values = raw.astype(F32)
    norm = jnp.sqrt(jnp.sum(values * values, axis=1, keepdims=True) + EPS)
    return values / norm, norm


def image_unit_kernel(scale_ref, raw_ref, text_ref, out_ref, pairs_ref, raw, text, unit, sem):
    copies = run([
        pltpu.make_async_copy(raw_ref, raw, sem.at[0]), pltpu.make_async_copy(text_ref, text, sem.at[1])
    ])
    copies[0].wait()
    unit[...] = unit_rows(raw[...])[0].astype(BF16)
    out = run([pltpu.make_async_copy(unit, out_ref, sem.at[2])])
    copies[1].wait()
    other = unit_rows(text[...])[0].astype(BF16)
    total = jnp.sum(unit[...].astype(F32) * other.astype(F32), keepdims=True)
    pairs_ref[...] = jnp.broadcast_to(total * (scale_ref[0] * LOG2E), pairs_ref.shape)
    wait(out)


def text_units_kernel(raw_ref, out_ref, raw, unit, sem):
    wait(run([pltpu.make_async_copy(raw_ref, raw, sem.at[0])]))
    unit[...] = unit_rows(raw[...])[0].astype(BF16)
    wait(run([
        pltpu.make_async_copy(unit, out_ref.at[pl.ds(k * PIECE, PIECE), :], sem.at[k])
        for k in range(PEERS)
    ]))


def to_lanes(column):
    return jnp.broadcast_to(column, (column.shape[0], 128)).T[:1, :]


def to_rows(lanes):
    return jnp.broadcast_to(lanes, (128, lanes.shape[1])).T[:, :1]


def logits_kernel(plan, at_ref, scale_ref, text_ref, *refs):
    pieces = refs[: len(plan)]
    image_out, logits_ref, keep_ref, give_ref, image_ref, sem, out_sem = refs[len(plan) :]
    core = at_ref[2]
    copies = []
    for k, (piece, (flip, by, start, rows)) in enumerate(zip(pieces, plan)):
        block = lax.rem(at_ref[3] + by + DEEP, DEEP)
        first = pl.multiple_of(flip * (SIDE // 2) + block * PIECE + start, 32)
        copies.append(pltpu.make_async_copy(piece, image_ref.at[pl.ds(first, rows), :], sem.at[k]))
    near = len(plan) // 2
    halves = [pl.ds(k * (SIDE // 2), SIDE // 2) for k in range(2)]
    out = [pltpu.make_async_copy(image_ref.at[h, :], image_out.at[h, :], out_sem.at[k]) for k, h in enumerate(halves)]
    wait(run(copies[:near]))
    run(copies[near:] + out[:1])
    text = text_ref[...]
    scale = scale_ref[0] * LOG2E
    top = jnp.full((1, SIDE), LOW, F32)
    sums = jnp.zeros((1, SIDE), F32)
    row_lse = []
    for k in range(STEPS):
        if k == STEPS // 2:
            wait(copies[near:])
            run(out[1:])
        tile = slice(k * TILE, (k + 1) * TILE)
        logits = scale * lax.dot_general(
            image_ref[tile, :], text, (((1,), (1,)), ((), ())), preferred_element_type=F32
        )
        logits_ref[tile, :] = logits
        row_top = jnp.max(logits, axis=1, keepdims=True)
        row_sum = jnp.sum(jnp.exp2(logits - row_top), axis=1, keepdims=True)
        row_lse.append(to_lanes(row_top + jnp.log2(row_sum)))
        new = jnp.maximum(top, jnp.max(logits, axis=0, keepdims=True))
        sums = sums * jnp.exp2(top - new) + jnp.sum(jnp.exp2(logits - new), axis=0, keepdims=True)
        top = new
    col_lse = top + jnp.log2(sums)
    first = core == 0
    for k in range(STEPS):
        part = col_lse[:, k * TILE : (k + 1) * TILE]
        keep_ref[k : k + 1, :] = jnp.where(first, part, row_lse[k])
        give_ref[k : k + 1, :] = jnp.where(first, row_lse[(k + STEPS // 2) % STEPS], part)
    wait(out)


def spread_kernel(at_ref, keep_ref, recv_ref, ours_ref, theirs_ref, out_ref):
    keep, recv = keep_ref[...], recv_ref[...]
    top = jnp.maximum(keep, recv)
    both = top + jnp.log2(jnp.exp2(keep - top) + jnp.exp2(recv - top))
    pairs = jnp.broadcast_to(ours_ref[:1, :1] + theirs_ref[:1, :1], (2 * STEPS, TILE))
    first = at_ref[2] == 0
    block = jnp.concatenate([jnp.where(first, keep, both), jnp.where(first, recv, both), pairs], axis=0)
    for k in range(PEERS):
        out_ref[pl.ds(k * LINES, LINES), :] = block


def join_kernel(at_ref, parts_ref, keep_ref, give_ref):
    parts = parts_ref[...].reshape(PEERS, LINES, TILE)
    pairs = jnp.sum(parts[:, 2 * STEPS : 2 * STEPS + 1, :1], axis=0)
    parts = parts[:, : 2 * STEPS, :]
    half = lax.broadcasted_iota(jnp.int32, parts.shape, 0) // DEEP
    first = at_ref[2] == 0
    parts = jnp.where(first | (half == at_ref[4]), parts, LOW)
    top = jnp.max(parts, axis=0)
    lse = top + jnp.log2(jnp.sum(jnp.exp2(parts - top[None]), axis=0))
    columns = jnp.broadcast_to(jnp.sum(lse, keepdims=True) - 2.0 * pairs, (STEPS, TILE))
    keep_ref[:STEPS, :] = lse[:STEPS]
    keep_ref[STEPS:, :] = columns
    turned = jnp.concatenate([lse[STEPS // 2 : STEPS], lse[: STEPS // 2]], axis=0)
    give_ref[:STEPS, :] = jnp.where(first, lse[STEPS:], turned)
    give_ref[STEPS:, :] = columns


def tag(term, rows=PIECE):
    term = jnp.broadcast_to(term, (rows, 128))
    high = term.astype(BF16).astype(F32)
    middle = (term - high).astype(BF16).astype(F32)
    low = (term - high) - middle
    lane = lax.rem(lax.broadcasted_iota(jnp.int32, (rows, 128), 1), 4)
    return jnp.where(lane == 0, high, jnp.where(lane == 1, middle, low)).astype(BF16)


def place_tag(at_ref, sums_ref):
    lane = lax.broadcasted_iota(jnp.int32, (1, 128), 1)
    mark = tag(sums_ref[STEPS : STEPS + 1, :1], 16).astype(F32)[:1]
    return jnp.where(lane // 4 == at_ref[3], mark, 0.0)


def untag(row, lane=0):
    return (row[:, lane : lane + 1] + row[:, lane + 1 : lane + 2]) + row[:, lane + 2 : lane + 3]


def weights_kernel(
    at_ref, scale_ref, logits_ref, text_ref, keep_ref, recv_ref,
    weights_ref, turned_ref, other_ref, sums_ref,
):
    first = at_ref[2] == 0
    keep, recv = keep_ref[:STEPS, :], recv_ref[:STEPS, :]
    cols = jnp.where(first, keep, recv)
    col_lse = jnp.concatenate([cols[k : k + 1] for k in range(STEPS)], axis=1)
    rows = jnp.where(first, recv, keep)
    sums_ref[:STEPS, :] = jnp.broadcast_to(jnp.sum(rows, keepdims=True), (STEPS, 128))
    sums_ref[STEPS:, :] = jnp.where(first, keep_ref[STEPS:, :128], recv_ref[STEPS:, :128])
    row_at = lax.broadcasted_iota(jnp.int32, (TILE, 1), 0) - at_ref[3] * PIECE
    col_at = lax.broadcasted_iota(jnp.int32, (1, SIDE), 1) - at_ref[1] * PIECE
    col_at = jnp.where((col_at >= 0) & (col_at < PIECE), col_at, -SIDE)
    text = text_ref[...]
    for k in (2, 3, 0, 1):
        tile = slice(k * TILE, (k + 1) * TILE)
        logits = logits_ref[tile, :]
        weights = jnp.exp2(logits - to_rows(rows[k : k + 1])) + jnp.exp2(logits - col_lse)
        if k < STEPS // 2:
            weights -= jnp.where(row_at + k * TILE == col_at, 2.0, 0.0)
        weights = (weights * 0.5).astype(BF16)
        turned_ref[:, tile] = weights.T
        if k < STEPS // 2:
            weights_ref[tile, :] = weights
        else:
            other_ref[(k - 2) * TILE : (k - 1) * TILE, :] = (
                scale_ref[0] * jnp.dot(weights, text, preferred_element_type=F32)
            ).astype(BF16)


def back_tile(k, scale_ref, turned_ref, image, mark, out_ref):
    tile = slice(k * TILE, (k + 1) * TILE)
    term = (
        scale_ref[0] * jnp.dot(turned_ref[tile, :], image, preferred_element_type=F32)
    ).astype(BF16)
    peers = TILE // PIECE
    for p in range(peers):
        start = (k * peers + p) * PART
        for b in range(WIDTH // 128):
            out_ref[start + b * PIECE : start + (b + 1) * PIECE, :] = (
                term[p * PIECE : (p + 1) * PIECE, b * 128 : (b + 1) * 128]
            )
        out_ref[start + PART - MARK : start + PART, :] = mark


EARLY = 3
SPLIT = EARLY * (TILE // PIECE) * PART


def text_back_kernel(scale_ref, turned_ref, image_ref, sums_ref, out_ref):
    image = image_ref[...]
    mark = tag(sums_ref[:1, :1], MARK)
    for k in range(EARLY):
        back_tile(k, scale_ref, turned_ref, image, mark, out_ref)


HALF = PIECE // 2
AWAY = (3, 2, 1, -3, -2, -1)


def pieces_kernel(
    at_ref, scale_ref, weights_ref, turned_ref, image_ref, text_ref, sums_ref, swapped_ref, begun_ref, out_ref, *refs
):
    own_out, up_out, down_out, *away_refs, mine, parts, ends, back, sem, back_sem = refs
    begun = run([pltpu.make_async_copy(begun_ref, out_ref.at[pl.ds(0, SPLIT), :], back_sem.at[0])])
    mine[...] = scale_ref[0] * jnp.dot(
        weights_ref[...], text_ref[...], preferred_element_type=F32
    ) + swapped_ref[...].astype(F32)

    def block(by):
        return pl.ds(pl.multiple_of(lax.rem(at_ref[3] + by + DEEP, DEEP) * PIECE, PIECE), PIECE)

    ends[:, :WIDTH] = mine[block(4), :].astype(BF16)
    ends[:, WIDTH:] = jnp.broadcast_to(place_tag(at_ref, sums_ref), (PIECE, 128)).astype(BF16)
    copies = run([
        pltpu.make_async_copy(ends.at[pl.ds(0, HALF), :], up_out, sem.at[0]),
        pltpu.make_async_copy(ends.at[pl.ds(HALF, HALF), :], down_out, sem.at[1]),
        pltpu.make_async_copy(mine.at[block(0), :], own_out, sem.at[2]),
    ])
    for k, (by, ref) in enumerate(zip(AWAY, away_refs)):
        parts[k] = mine[block(by), :].astype(BF16)
        copies += run([pltpu.make_async_copy(parts.at[k], ref, sem.at[3 + k])])
    for k in range(EARLY, STEPS):
        back_tile(k - EARLY, scale_ref, turned_ref.at[pl.ds(EARLY * TILE, SIDE - EARLY * TILE), :], image_ref[...], tag(sums_ref[:1, :1], MARK), back)
    begun += run([
        pltpu.make_async_copy(back, out_ref.at[pl.ds(SPLIT, PEERS * PART - SPLIT), :], back_sem.at[1])
    ])
    wait(begun + copies)


def relay_kernel(
    at_ref, sums_ref, up_ref, down_ref, below_ref, above_ref, up_out, down_out, up, down, sem
):
    copies = run([pltpu.make_async_copy(up_ref, up, sem.at[0]), pltpu.make_async_copy(down_ref, down, sem.at[1])])
    mark = place_tag(at_ref, sums_ref)
    for k, (copy, ours, theirs, out) in enumerate(
        zip(copies, (up, down), (below_ref, above_ref), (up_out, down_out))
    ):
        came = theirs[:, :WIDTH].astype(F32)
        if came.shape[0] == HALF:
            rest = jnp.zeros_like(came)
            came = jnp.concatenate([came, rest] if k == 0 else [rest, came], axis=0)
        marks = theirs[:16, WIDTH:].astype(F32)[:1] + mark
        out[:, WIDTH:] = jnp.broadcast_to(marks, (PIECE, 128)).astype(BF16)
        copy.wait()
        out[:, :WIDTH] = (ours[...].astype(F32) + came).astype(BF16)


def project(back, raw):
    direction, norm = unit_rows(raw)
    along = jnp.sum(direction * back, axis=1, keepdims=True)
    return ((back - direction * along) / norm).astype(BF16)


def text_grad_kernel(raw_ref, loss_ref, parts_ref, out_ref, total_ref, raw, grad, sem):
    copies = run([pltpu.make_async_copy(raw_ref, raw, sem.at[0])])
    total = loss_ref[:1, :1]
    for k in range(PEERS):
        total += untag(parts_ref[(k + 1) * PART - MARK : (k + 1) * PART, :].astype(F32)[:1])
    total_ref[0] = (total * (LN2 / (2.0 * SIDE * PEERS)))[0, 0]
    columns = []
    for b in range(WIDTH // 128):
        column = jnp.zeros((PIECE, 128), F32)
        for k in range(PEERS):
            start = k * PART + b * PIECE
            column += parts_ref[start : start + PIECE, :].astype(F32)
        columns.append(column)
    wait(copies)
    grad[...] = project(jnp.concatenate(columns, axis=1), raw[...])
    wait(run([pltpu.make_async_copy(grad, out_ref, sem.at[0])]))


def image_grad_kernel(at_ref, sums_ref, raw_ref, own_ref, below_ref, above_ref, out_ref, loss_ref, raw, own, grad, sem):
    copies = run([
        pltpu.make_async_copy(raw_ref, raw, sem.at[0]), pltpu.make_async_copy(own_ref, own, sem.at[1])
    ])
    twice = lax.rem(at_ref[3] + DEEP // 2, DEEP)
    lane = lax.broadcasted_iota(jnp.int32, (1, 128), 1)
    marks = place_tag(at_ref, sums_ref) + below_ref[:16, WIDTH:].astype(F32)[:1]
    marks += jnp.where(lane // 4 == twice, 0.0, above_ref[:16, WIDTH:].astype(F32)[:1])
    total = jnp.zeros((1, 1), F32)
    for k in range(DEEP):
        total += untag(marks, 4 * k)
    loss_ref[...] = jnp.broadcast_to(total, loss_ref.shape)
    wait(copies)
    back = own[...] + below_ref[:, :WIDTH].astype(F32) + above_ref[:, :WIDTH].astype(F32)
    grad[...] = project(back, raw[...])
    wait(run([pltpu.make_async_copy(grad, out_ref, sem.at[0])]))


def gather_image(unit):
    plan, arrays = [(0, 0, 0, PIECE)], [unit]
    up, down, half = unit, unit, PIECE // 2
    for by in range(1, DEEP // 2):
        up, down = send(up, "z", 1), send(down, "z", -1)
        plan += [(0, -by, 0, PIECE), (0, by, 0, PIECE)]
        arrays += [up, down]
    plan += [(0, -(DEEP // 2), 0, half), (0, DEEP // 2, half, half)]
    arrays += [send(up[:half], "z", 1), send(down[half:], "z", -1)]
    plan += [(1, *rest) for _, *rest in plan]
    arrays += [send(a, "c", 1) for a in arrays]
    return plan, arrays


def body(image_emb, text_emb, log_scale):
    width = image_emb.shape[1]
    scale = jnp.exp(log_scale)
    me = lax.axis_index("d")
    z, core, x = me % 8, (me // 8) % 2, me // 64
    at = jnp.stack([me % 16, me // 16, core, z, x % 2]).astype(jnp.int32)
    piece = local((PIECE, width), BF16)
    side = local((SIDE, width), BF16)
    outside = array((SIDE, width), BF16)
    raw = pltpu.VMEM((PIECE, width), BF16)
    sems = pltpu.SemaphoreType.DMA

    image_unit, pairs = call(
        image_unit_kernel, [array((PIECE, width), BF16), local((8, 128), F32)],
        scale, Outside(image_emb), Outside(text_emb), scratch=[raw, raw, raw, sems((3,))],
    )
    plan, pieces = gather_image(image_unit)
    text_units = call(text_units_kernel, outside, Outside(text_emb), scratch=[raw, raw, sems((PEERS,))])
    text = exchange(text_units, XY)

    pairs = [pairs, send(pairs, "c", 1)]

    lines = local((STEPS, TILE), F32)
    image, logits, keep, give = call(
        functools.partial(logits_kernel, plan), [outside, local((SIDE, SIDE), F32), lines, lines],
        at, scale, text, *map(Outside, pieces),
        scratch=[pltpu.VMEM((SIDE, width), BF16), sems((len(plan),)), sems((2,))],
    )
    spread = call(spread_kernel, local((PEERS * LINES, TILE), F32), at, keep, send(give, "c", 1), *pairs)
    lines = local((2 * STEPS, TILE), F32)
    keep, give = call(join_kernel, [lines, lines], at, exchange(spread, MIXED))
    recv = send(give, "c", 1)

    half = (SIDE // 2, width)
    weights, turned, other, sums = call(
        weights_kernel,
        [local((SIDE // 2, SIDE), BF16), local((SIDE, SIDE), BF16), local(half, BF16), local((2 * STEPS, 128), F32)],
        at, scale, logits, text, keep, recv,
    )
    swapped = send(other, "c", 1)
    text_parts = call(text_back_kernel, local((SPLIT, 128), BF16), scale, turned, image, sums)
    end = array((HALF, WIDER), BF16)
    away = [array((PIECE, width), BF16)] * len(AWAY)
    text_parts, own, up, down, *away = call(
        pieces_kernel, [array((PEERS * PART, 128), BF16), array((PIECE, width), F32), end, end, *away],
        at, scale, weights, turned, image, text, sums, swapped, text_parts,
        scratch=[
            pltpu.VMEM(half, F32),
            pltpu.VMEM((len(AWAY), PIECE, width), BF16),
            pltpu.VMEM((PIECE, WIDER), BF16),
            pltpu.VMEM((PEERS * PART - SPLIT, 128), BF16),
            sems((3 + len(AWAY),)),
            sems((2,)),
        ],
    )
    text_back = exchange(text_parts, XY)
    below, above = send(up, "z", 1), send(down, "z", -1)
    whole = local((PIECE, WIDER), BF16)
    for k in range(3):
        up, down = call(
            relay_kernel, [whole] * 2, at, sums, Outside(away[k]), Outside(away[k + 3]), below, above,
            scratch=[raw, raw, sems((2,))],
        )
        below, above = send(up, "z", 1), send(down, "z", -1)

    grad = array((PIECE, width), BF16)
    grad_image, part = call(
        image_grad_kernel, [grad, local((8, 128), F32)],
        at, sums, Outside(image_emb), Outside(own), below, above,
        scratch=[raw, pltpu.VMEM((PIECE, width), F32), raw, sems((2,))],
    )
    grad_text, loss = call(
        text_grad_kernel, [grad, pltpu.SMEM((1,), F32)], Outside(text_emb), part, text_back,
        scratch=[raw, raw, sems((1,))],
    )
    return loss, grad_image, grad_text


def solution(mesh):
    flat = Mesh(mesh.devices.reshape(-1), ("d",))
    return jax.shard_map(
        body,
        mesh=flat,
        in_specs=(P("d", None), P("d", None), P()),
        out_specs=(P(), P("d", None), P("d", None)),
        check_vma=False,
    )
```

```python
import functools
import math
import typing

import jax
import jax.numpy as jnp
import numpy as np
from jax import lax
from jax.experimental import pallas as pl
from jax.experimental.pallas import tpu as pltpu
from jax.sharding import Mesh, PartitionSpec as P

LOG2E = math.log2(math.e)
LN2 = math.log(2.0)
EPS = 1e-06
LOW = -1e30
PARAMS = pltpu.CompilerParams(vmem_limit_bytes=24 * 1024 * 1024)
HBM = pl.BlockSpec(memory_space=pl.ANY)
WHOLE = pl.BlockSpec(memory_space=pltpu.VMEM)
SCALAR = pl.BlockSpec(memory_space=pltpu.SMEM)
F32 = jnp.float32
BF16 = jnp.bfloat16

INDEX = np.arange(256).reshape(4, 4, 2, 8)
AXES = {"x": 0, "y": 1, "c": 2, "z": 3}
XY = INDEX.transpose(2, 3, 0, 1).reshape(16, 16).tolist()
MIXED = INDEX[:, :, 0, :].transpose(2, 0, 1).reshape(8, 16).tolist() + (
    INDEX[:, :, 1, :].reshape(2, 2, 4, 8).transpose(0, 2, 1, 3).reshape(8, 16).tolist()
)
PEERS = 16
PIECE = 64
SIDE = PEERS * PIECE
TILE = 256
STEPS = SIDE // TILE
DEEP = 8
LINES = 2 * STEPS
WIDTH = 1280
WIDER = WIDTH + 128
MARK = 16
PART = PIECE * (WIDTH // 128) + MARK


def shift(axis, by):
    to = np.roll(INDEX, -by, AXES[axis])
    return [(int(a), int(b)) for a, b in zip(INDEX.ravel(), to.ravel())]


def send(x, axis, by):
    return lax.ppermute(x, "d", shift(axis, by))


def exchange(x, groups):
    return lax.all_to_all(x, "d", 0, 0, axis_index_groups=groups, tiled=True)


def array(shape, dtype):
    return pltpu.HBM(shape, dtype)


def local(shape, dtype):
    return pltpu.VMEM(shape, dtype)


def call(kernel, outputs, *operands, scratch=(), aliases={}):
    specs, arrays = [], []
    for x in operands:
        if isinstance(x, Outside):
            specs.append(HBM)
            arrays.append(pltpu.with_memory_space_constraint(x.array, pltpu.HBM))
        elif x.size <= 8:
            specs.append(SCALAR)
            arrays.append(x)
        else:
            specs.append(WHOLE)
            arrays.append(pltpu.with_memory_space_constraint(x, pltpu.VMEM))
    return pl.pallas_call(
        kernel,
        out_shape=outputs,
        in_specs=specs,
        out_specs=jax.tree.map(lambda s: {pltpu.VMEM: WHOLE, pltpu.SMEM: SCALAR}.get(s.memory_space, HBM), outputs),
        scratch_shapes=list(scratch),
        input_output_aliases=aliases,
        compiler_params=PARAMS,
    )(*arrays)


class Outside(typing.NamedTuple):
    array: typing.Any


def run(copies):
    for copy in copies:
        copy.start()
    return copies


def wait(copies):
    for copy in copies:
        copy.wait()


def unit_rows(raw):
    values = raw.astype(F32)
    norm = jnp.sqrt(jnp.sum(values * values, axis=1, keepdims=True) + EPS)
    return values / norm, norm


def image_unit_kernel(scale_ref, raw_ref, text_ref, out_ref, pairs_ref, raw, text, unit, sem):
    copies = run([
        pltpu.make_async_copy(raw_ref, raw, sem.at[0]), pltpu.make_async_copy(text_ref, text, sem.at[1])
    ])
    copies[0].wait()
    unit[...] = unit_rows(raw[...])[0].astype(BF16)
    out = run([pltpu.make_async_copy(unit, out_ref, sem.at[2])])
    copies[1].wait()
    other = unit_rows(text[...])[0].astype(BF16)
    total = jnp.sum(unit[...].astype(F32) * other.astype(F32), keepdims=True)
    pairs_ref[...] = jnp.broadcast_to(total * (scale_ref[0] * LOG2E), pairs_ref.shape)
    wait(out)


def text_units_kernel(raw_ref, out_ref, raw, unit, sem):
    wait(run([pltpu.make_async_copy(raw_ref, raw, sem.at[0])]))
    unit[...] = unit_rows(raw[...])[0].astype(BF16)
    wait(run([
        pltpu.make_async_copy(unit, out_ref.at[pl.ds(k * PIECE, PIECE), :], sem.at[k])
        for k in range(PEERS)
    ]))


def to_lanes(column):
    return jnp.broadcast_to(column, (column.shape[0], 128)).T[:1, :]


def to_rows(lanes):
    return jnp.broadcast_to(lanes, (128, lanes.shape[1])).T[:, :1]


def logits_kernel(plan, at_ref, scale_ref, text_ref, *refs):
    pieces = refs[: len(plan)]
    image_out, logits_ref, keep_ref, give_ref, image_ref, sem, out_sem = refs[len(plan) :]
    core = at_ref[2]
    copies = []
    for k, (piece, (flip, by, start, rows)) in enumerate(zip(pieces, plan)):
        block = lax.rem(at_ref[3] + by + DEEP, DEEP)
        first = pl.multiple_of(flip * (SIDE // 2) + block * PIECE + start, 32)
        copies.append(pltpu.make_async_copy(piece, image_ref.at[pl.ds(first, rows), :], sem.at[k]))
    near = len(plan) // 2
    halves = [pl.ds(k * (SIDE // 2), SIDE // 2) for k in range(2)]
    out = [pltpu.make_async_copy(image_ref.at[h, :], image_out.at[h, :], out_sem.at[k]) for k, h in enumerate(halves)]
    wait(run(copies[:near]))
    run(copies[near:] + out[:1])
    text = text_ref[...]
    scale = scale_ref[0] * LOG2E
    top = jnp.full((1, SIDE), LOW, F32)
    sums = jnp.zeros((1, SIDE), F32)
    row_lse = []
    for k in range(STEPS):
        if k == STEPS // 2:
            wait(copies[near:])
            run(out[1:])
        tile = slice(k * TILE, (k + 1) * TILE)
        logits = scale * lax.dot_general(
            image_ref[tile, :], text, (((1,), (1,)), ((), ())), preferred_element_type=F32
        )
        logits_ref[tile, :] = logits
        row_top = jnp.max(logits, axis=1, keepdims=True)
        row_sum = jnp.sum(jnp.exp2(logits - row_top), axis=1, keepdims=True)
        row_lse.append(to_lanes(row_top + jnp.log2(row_sum)))
        new = jnp.maximum(top, jnp.max(logits, axis=0, keepdims=True))
        sums = sums * jnp.exp2(top - new) + jnp.sum(jnp.exp2(logits - new), axis=0, keepdims=True)
        top = new
    col_lse = top + jnp.log2(sums)
    first = core == 0
    for k in range(STEPS):
        part = col_lse[:, k * TILE : (k + 1) * TILE]
        keep_ref[k : k + 1, :] = jnp.where(first, part, row_lse[k])
        give_ref[k : k + 1, :] = jnp.where(first, row_lse[(k + STEPS // 2) % STEPS], part)
    wait(out)


def spread_kernel(at_ref, keep_ref, recv_ref, ours_ref, theirs_ref, out_ref):
    keep, recv = keep_ref[...], recv_ref[...]
    top = jnp.maximum(keep, recv)
    both = top + jnp.log2(jnp.exp2(keep - top) + jnp.exp2(recv - top))
    pairs = jnp.broadcast_to(ours_ref[:1, :1] + theirs_ref[:1, :1], (STEPS, TILE))
    first = at_ref[2] == 0
    block = jnp.concatenate([jnp.where(first, keep, both), jnp.where(first, recv, pairs)], axis=0)
    for k in range(PEERS):
        out_ref[pl.ds(k * LINES, LINES), :] = block


def join_kernel(at_ref, parts_ref, keep_ref, give_ref):
    parts = parts_ref[...].reshape(PEERS, LINES, TILE)
    half = lax.broadcasted_iota(jnp.int32, parts.shape, 0) // DEEP
    first = at_ref[2] == 0
    used = first | (half == at_ref[4])
    pairs = jnp.sum(jnp.where(used, parts, 0.0)[:, STEPS:, :1], axis=0)[:1]
    parts = jnp.where(used, parts, LOW)
    top = jnp.max(parts, axis=0)
    lse = top + jnp.log2(jnp.sum(jnp.exp2(parts - top[None]), axis=0))
    low = jnp.sum(lse[:STEPS], keepdims=True)
    high = jnp.sum(lse[STEPS:], keepdims=True)
    term = jnp.broadcast_to(jnp.where(first, low + high, low - 2.0 * pairs), (STEPS, TILE))
    keep_ref[:STEPS, :] = lse[:STEPS]
    keep_ref[STEPS:, :] = term
    turned = jnp.concatenate([lse[STEPS // 2 : STEPS], lse[: STEPS // 2]], axis=0)
    give_ref[:STEPS, :] = jnp.where(first, lse[STEPS:], turned)
    give_ref[STEPS:, :] = term


def tag(term, rows=PIECE):
    term = jnp.broadcast_to(term, (rows, 128))
    high = term.astype(BF16).astype(F32)
    middle = (term - high).astype(BF16).astype(F32)
    low = (term - high) - middle
    lane = lax.rem(lax.broadcasted_iota(jnp.int32, (rows, 128), 1), 4)
    return jnp.where(lane == 0, high, jnp.where(lane == 1, middle, low)).astype(BF16)


def place_tag(at_ref, sums_ref):
    lane = lax.broadcasted_iota(jnp.int32, (1, 128), 1)
    mark = tag(sums_ref[STEPS : STEPS + 1, :1], 16).astype(F32)[:1]
    return jnp.where(lane // 4 == at_ref[3], mark, 0.0)


def untag(row, lane=0):
    return (row[:, lane : lane + 1] + row[:, lane + 1 : lane + 2]) + row[:, lane + 2 : lane + 3]


def weights_kernel(
    at_ref, scale_ref, logits_ref, text_ref, keep_ref, recv_ref,
    weights_ref, turned_ref, other_ref, sums_ref,
):
    first = at_ref[2] == 0
    keep, recv = keep_ref[:STEPS, :], recv_ref[:STEPS, :]
    cols = jnp.where(first, keep, recv)
    col_lse = jnp.concatenate([cols[k : k + 1] for k in range(STEPS)], axis=1)
    rows = jnp.where(first, recv, keep)
    sums_ref[:STEPS, :] = jnp.where(first, recv_ref[STEPS:, :128], keep_ref[STEPS:, :128])
    sums_ref[STEPS:, :] = jnp.where(first, keep_ref[STEPS:, :128], recv_ref[STEPS:, :128])
    row_at = lax.broadcasted_iota(jnp.int32, (TILE, 1), 0) - at_ref[3] * PIECE
    col_at = lax.broadcasted_iota(jnp.int32, (1, SIDE), 1) - at_ref[1] * PIECE
    col_at = jnp.where((col_at >= 0) & (col_at < PIECE), col_at, -SIDE)
    text = text_ref[...]
    for k in (2, 3, 0, 1):
        tile = slice(k * TILE, (k + 1) * TILE)
        logits = logits_ref[tile, :]
        weights = jnp.exp2(logits - to_rows(rows[k : k + 1])) + jnp.exp2(logits - col_lse)
        if k < STEPS // 2:
            weights -= jnp.where(row_at + k * TILE == col_at, 2.0, 0.0)
        weights = (weights * 0.5).astype(BF16)
        turned_ref[:, tile] = weights.T
        if k < STEPS // 2:
            weights_ref[tile, :] = weights
        else:
            other_ref[(k - 2) * TILE : (k - 1) * TILE, :] = (
                scale_ref[0] * jnp.dot(weights, text, preferred_element_type=F32)
            ).astype(BF16)


def back_tile(k, scale_ref, turned_ref, image, mark, out_ref):
    tile = slice(k * TILE, (k + 1) * TILE)
    term = (
        scale_ref[0] * jnp.dot(turned_ref[tile, :], image, preferred_element_type=F32)
    ).astype(BF16)
    peers = TILE // PIECE
    for p in range(peers):
        start = (k * peers + p) * PART
        for b in range(WIDTH // 128):
            out_ref[start + b * PIECE : start + (b + 1) * PIECE, :] = (
                term[p * PIECE : (p + 1) * PIECE, b * 128 : (b + 1) * 128]
            )
        out_ref[start + PART - MARK : start + PART, :] = mark


EARLY = 4
SPLIT = EARLY * (TILE // PIECE) * PART


def text_back_kernel(scale_ref, turned_ref, image_ref, sums_ref, out_ref):
    image = image_ref[...]
    mark = tag(sums_ref[:1, :1], MARK)
    for k in range(EARLY):
        back_tile(k, scale_ref, turned_ref, image, mark, out_ref)


HALF = PIECE // 2
AWAY = (3, 2, 1, -3, -2, -1)


def pieces_kernel(
    at_ref, scale_ref, weights_ref, text_ref, sums_ref, swapped_ref, begun_ref, out_ref, *refs
):
    own_out, up_out, down_out, *away_refs, mine, parts, ends, sem, back_sem = refs
    begun = run([pltpu.make_async_copy(begun_ref, out_ref, back_sem.at[0])])
    mine[...] = scale_ref[0] * jnp.dot(
        weights_ref[...], text_ref[...], preferred_element_type=F32
    ) + swapped_ref[...].astype(F32)

    def block(by):
        return pl.ds(pl.multiple_of(lax.rem(at_ref[3] + by + DEEP, DEEP) * PIECE, PIECE), PIECE)

    ends[:, :WIDTH] = mine[block(4), :].astype(BF16)
    ends[:, WIDTH:] = jnp.broadcast_to(place_tag(at_ref, sums_ref), (PIECE, 128)).astype(BF16)
    copies = run([
        pltpu.make_async_copy(ends.at[pl.ds(0, HALF), :], up_out, sem.at[0]),
        pltpu.make_async_copy(ends.at[pl.ds(HALF, HALF), :], down_out, sem.at[1]),
        pltpu.make_async_copy(mine.at[block(0), :], own_out, sem.at[2]),
    ])
    for k, (by, ref) in enumerate(zip(AWAY, away_refs)):
        parts[k] = mine[block(by), :].astype(BF16)
        copies += run([pltpu.make_async_copy(parts.at[k], ref, sem.at[3 + k])])
    wait(begun + copies)


def relay_kernel(
    at_ref, sums_ref, up_ref, down_ref, below_ref, above_ref, up_out, down_out, up, down, sem
):
    copies = run([pltpu.make_async_copy(up_ref, up, sem.at[0]), pltpu.make_async_copy(down_ref, down, sem.at[1])])
    mark = place_tag(at_ref, sums_ref)
    for k, (copy, ours, theirs, out) in enumerate(
        zip(copies, (up, down), (below_ref, above_ref), (up_out, down_out))
    ):
        came = theirs[:, :WIDTH].astype(F32)
        if came.shape[0] == HALF:
            rest = jnp.zeros_like(came)
            came = jnp.concatenate([came, rest] if k == 0 else [rest, came], axis=0)
        marks = theirs[:16, WIDTH:].astype(F32)[:1] + mark
        out[:, WIDTH:] = jnp.broadcast_to(marks, (PIECE, 128)).astype(BF16)
        copy.wait()
        out[:, :WIDTH] = (ours[...].astype(F32) + came).astype(BF16)


def project(back, raw):
    direction, norm = unit_rows(raw)
    along = jnp.sum(direction * back, axis=1, keepdims=True)
    return ((back - direction * along) / norm).astype(BF16)


def text_grad_kernel(raw_ref, loss_ref, parts_ref, out_ref, total_ref, raw, grad, sem):
    copies = run([pltpu.make_async_copy(raw_ref, raw, sem.at[0])])
    total = loss_ref[:1, :1]
    for k in range(PEERS):
        total += untag(parts_ref[(k + 1) * PART - MARK : (k + 1) * PART, :].astype(F32)[:1])
    total_ref[0] = (total * (LN2 / (2.0 * SIDE * PEERS)))[0, 0]
    columns = []
    for b in range(WIDTH // 128):
        column = jnp.zeros((PIECE, 128), F32)
        for k in range(PEERS):
            start = k * PART + b * PIECE
            column += parts_ref[start : start + PIECE, :].astype(F32)
        columns.append(column)
    wait(copies)
    grad[...] = project(jnp.concatenate(columns, axis=1), raw[...])
    wait(run([pltpu.make_async_copy(grad, out_ref, sem.at[0])]))


def image_grad_kernel(at_ref, sums_ref, raw_ref, own_ref, below_ref, above_ref, out_ref, loss_ref, raw, own, grad, sem):
    copies = run([
        pltpu.make_async_copy(raw_ref, raw, sem.at[0]), pltpu.make_async_copy(own_ref, own, sem.at[1])
    ])
    twice = lax.rem(at_ref[3] + DEEP // 2, DEEP)
    lane = lax.broadcasted_iota(jnp.int32, (1, 128), 1)
    marks = place_tag(at_ref, sums_ref) + below_ref[:16, WIDTH:].astype(F32)[:1]
    marks += jnp.where(lane // 4 == twice, 0.0, above_ref[:16, WIDTH:].astype(F32)[:1])
    total = jnp.zeros((1, 1), F32)
    for k in range(DEEP):
        total += untag(marks, 4 * k)
    loss_ref[...] = jnp.broadcast_to(total, loss_ref.shape)
    wait(copies)
    back = own[...] + below_ref[:, :WIDTH].astype(F32) + above_ref[:, :WIDTH].astype(F32)
    grad[...] = project(back, raw[...])
    wait(run([pltpu.make_async_copy(grad, out_ref, sem.at[0])]))


def gather_image(unit):
    plan, arrays = [(0, 0, 0, PIECE)], [unit]
    up, down, half = unit, unit, PIECE // 2
    for by in range(1, DEEP // 2):
        up, down = send(up, "z", 1), send(down, "z", -1)
        plan += [(0, -by, 0, PIECE), (0, by, 0, PIECE)]
        arrays += [up, down]
    plan += [(0, -(DEEP // 2), 0, half), (0, DEEP // 2, half, half)]
    arrays += [send(up[:half], "z", 1), send(down[half:], "z", -1)]
    plan += [(1, *rest) for _, *rest in plan]
    arrays += [send(a, "c", 1) for a in arrays]
    return plan, arrays


def body(image_emb, text_emb, log_scale):
    width = image_emb.shape[1]
    scale = jnp.exp(log_scale)
    me = lax.axis_index("d")
    z, core, x = me % 8, (me // 8) % 2, me // 64
    at = jnp.stack([me % 16, me // 16, core, z, x % 2]).astype(jnp.int32)
    piece = local((PIECE, width), BF16)
    side = local((SIDE, width), BF16)
    outside = array((SIDE, width), BF16)
    raw = pltpu.VMEM((PIECE, width), BF16)
    sems = pltpu.SemaphoreType.DMA

    image_unit, pairs = call(
        image_unit_kernel, [array((PIECE, width), BF16), local((8, 128), F32)],
        scale, Outside(image_emb), Outside(text_emb), scratch=[raw, raw, raw, sems((3,))],
    )
    plan, pieces = gather_image(image_unit)
    text_units = call(text_units_kernel, outside, Outside(text_emb), scratch=[raw, raw, sems((PEERS,))])
    text = exchange(text_units, XY)

    pairs = [pairs, send(pairs, "c", 1)]

    lines = local((STEPS, TILE), F32)
    image, logits, keep, give = call(
        functools.partial(logits_kernel, plan), [outside, local((SIDE, SIDE), F32), lines, lines],
        at, scale, text, *map(Outside, pieces),
        scratch=[pltpu.VMEM((SIDE, width), BF16), sems((len(plan),)), sems((2,))],
    )
    spread = call(spread_kernel, local((PEERS * LINES, TILE), F32), at, keep, send(give, "c", 1), *pairs)
    lines = local((2 * STEPS, TILE), F32)
    keep, give = call(join_kernel, [lines, lines], at, exchange(spread, MIXED))
    recv = send(give, "c", 1)

    half = (SIDE // 2, width)
    weights, turned, other, sums = call(
        weights_kernel,
        [local((SIDE // 2, SIDE), BF16), local((SIDE, SIDE), BF16), local(half, BF16), local((2 * STEPS, 128), F32)],
        at, scale, logits, text, keep, recv,
    )
    swapped = send(other, "c", 1)
    text_parts = call(text_back_kernel, local((SPLIT, 128), BF16), scale, turned, image, sums)
    end = array((HALF, WIDER), BF16)
    away = [array((PIECE, width), BF16)] * len(AWAY)
    text_parts, own, up, down, *away = call(
        pieces_kernel, [array((PEERS * PART, 128), BF16), array((PIECE, width), F32), end, end, *away],
        at, scale, weights, text, sums, swapped, text_parts,
        scratch=[
            pltpu.VMEM(half, F32),
            pltpu.VMEM((len(AWAY), PIECE, width), BF16),
            pltpu.VMEM((PIECE, WIDER), BF16),
            sems((3 + len(AWAY),)),
            sems((1,)),
        ],
    )
    text_back = exchange(text_parts, XY)
    below, above = send(up, "z", 1), send(down, "z", -1)
    whole = local((PIECE, WIDER), BF16)
    for k in range(3):
        up, down = call(
            relay_kernel, [whole] * 2, at, sums, Outside(away[k]), Outside(away[k + 3]), below, above,
            scratch=[raw, raw, sems((2,))],
        )
        below, above = send(up, "z", 1), send(down, "z", -1)

    grad = array((PIECE, width), BF16)
    grad_image, part = call(
        image_grad_kernel, [grad, local((8, 128), F32)],
        at, sums, Outside(image_emb), Outside(own), below, above,
        scratch=[raw, pltpu.VMEM((PIECE, width), F32), raw, sems((2,))],
    )
    grad_text, loss = call(
        text_grad_kernel, [grad, pltpu.SMEM((1,), F32)], Outside(text_emb), part, text_back,
        scratch=[raw, raw, sems((1,))],
    )
    return loss, grad_image, grad_text


def solution(mesh):
    flat = Mesh(mesh.devices.reshape(-1), ("d",))
    return jax.shard_map(
        body,
        mesh=flat,
        in_specs=(P("d", None), P("d", None), P()),
        out_specs=(P(), P("d", None), P("d", None)),
        check_vma=False,
    )
```

```python
import functools
import math
import typing

import jax
import jax.numpy as jnp
import numpy as np
from jax import lax
from jax.experimental import pallas as pl
from jax.experimental.pallas import tpu as pltpu
from jax.sharding import Mesh, PartitionSpec as P

LOG2E = math.log2(math.e)
LN2 = math.log(2.0)
EPS = 1e-06
LOW = -1e30
PARAMS = pltpu.CompilerParams(vmem_limit_bytes=24 * 1024 * 1024)
HBM = pl.BlockSpec(memory_space=pl.ANY)
WHOLE = pl.BlockSpec(memory_space=pltpu.VMEM)
SCALAR = pl.BlockSpec(memory_space=pltpu.SMEM)
F32 = jnp.float32
BF16 = jnp.bfloat16

INDEX = np.arange(256).reshape(4, 4, 2, 8)
AXES = {"x": 0, "y": 1, "c": 2, "z": 3}
XY = INDEX.transpose(2, 3, 0, 1).reshape(16, 16).tolist()
MIXED = INDEX[:, :, 0, :].transpose(2, 0, 1).reshape(8, 16).tolist() + (
    INDEX[:, :, 1, :].reshape(2, 2, 4, 8).transpose(0, 2, 1, 3).reshape(8, 16).tolist()
)
PEERS = 16
PIECE = 64
SIDE = PEERS * PIECE
TILE = 256
STEPS = SIDE // TILE
DEEP = 8
LINES = 2 * STEPS
WIDTH = 1280
MARK = 16
PART = PIECE * (WIDTH // 128) + MARK


def shift(axis, by):
    to = np.roll(INDEX, -by, AXES[axis])
    return [(int(a), int(b)) for a, b in zip(INDEX.ravel(), to.ravel())]


def send(x, axis, by):
    return lax.ppermute(x, "d", shift(axis, by))


def exchange(x, groups):
    return lax.all_to_all(x, "d", 0, 0, axis_index_groups=groups, tiled=True)


def array(shape, dtype):
    return pltpu.HBM(shape, dtype)


def local(shape, dtype):
    return pltpu.VMEM(shape, dtype)


def call(kernel, outputs, *operands, scratch=(), aliases={}):
    specs, arrays = [], []
    for x in operands:
        if isinstance(x, Outside):
            specs.append(HBM)
            arrays.append(pltpu.with_memory_space_constraint(x.array, pltpu.HBM))
        elif x.size <= 8:
            specs.append(SCALAR)
            arrays.append(x)
        else:
            specs.append(WHOLE)
            arrays.append(pltpu.with_memory_space_constraint(x, pltpu.VMEM))
    return pl.pallas_call(
        kernel,
        out_shape=outputs,
        in_specs=specs,
        out_specs=jax.tree.map(lambda s: {pltpu.VMEM: WHOLE, pltpu.SMEM: SCALAR}.get(s.memory_space, HBM), outputs),
        scratch_shapes=list(scratch),
        input_output_aliases=aliases,
        compiler_params=PARAMS,
    )(*arrays)


class Outside(typing.NamedTuple):
    array: typing.Any


def run(copies):
    for copy in copies:
        copy.start()
    return copies


def wait(copies):
    for copy in copies:
        copy.wait()


def unit_rows(raw):
    values = raw.astype(F32)
    norm = jnp.sqrt(jnp.sum(values * values, axis=1, keepdims=True) + EPS)
    return values / norm, norm


def image_unit_kernel(scale_ref, raw_ref, text_ref, out_ref, pairs_ref, raw, text, unit, sem):
    copies = run([
        pltpu.make_async_copy(raw_ref, raw, sem.at[0]), pltpu.make_async_copy(text_ref, text, sem.at[1])
    ])
    copies[0].wait()
    unit[...] = unit_rows(raw[...])[0].astype(BF16)
    out = run([pltpu.make_async_copy(unit, out_ref, sem.at[2])])
    copies[1].wait()
    other = unit_rows(text[...])[0].astype(BF16)
    total = jnp.sum(unit[...].astype(F32) * other.astype(F32), keepdims=True)
    pairs_ref[...] = jnp.broadcast_to(total * (scale_ref[0] * LOG2E), pairs_ref.shape)
    wait(out)


def text_units_kernel(raw_ref, out_ref, raw, unit, sem):
    wait(run([pltpu.make_async_copy(raw_ref, raw, sem.at[0])]))
    unit[...] = unit_rows(raw[...])[0].astype(BF16)
    wait(run([
        pltpu.make_async_copy(unit, out_ref.at[pl.ds(k * PIECE, PIECE), :], sem.at[k])
        for k in range(PEERS)
    ]))


def to_lanes(column):
    return jnp.broadcast_to(column, (column.shape[0], 128)).T[:1, :]


def to_rows(lanes):
    return jnp.broadcast_to(lanes, (128, lanes.shape[1])).T[:, :1]


def logits_kernel(plan, at_ref, scale_ref, pairs_ref, text_ref, *refs):
    pieces = refs[: len(plan)]
    image_out, logits_ref, keep_ref, give_ref, image_ref, sem, out_sem = refs[len(plan) :]
    core = at_ref[2]
    copies = []
    for k, (piece, (flip, by, start, rows)) in enumerate(zip(pieces, plan)):
        block = lax.rem(at_ref[3] + by + DEEP, DEEP)
        first = pl.multiple_of(flip * (SIDE // 2) + block * PIECE + start, 32)
        copies.append(pltpu.make_async_copy(piece, image_ref.at[pl.ds(first, rows), :], sem.at[k]))
    near = len(plan) // 2
    halves = [pl.ds(k * (SIDE // 2), SIDE // 2) for k in range(2)]
    out = [pltpu.make_async_copy(image_ref.at[h, :], image_out.at[h, :], out_sem.at[k]) for k, h in enumerate(halves)]
    wait(run(copies[:near]))
    run(copies[near:] + out[:1])
    text = text_ref[...]
    scale = scale_ref[0] * LOG2E
    top = jnp.full((1, SIDE), LOW, F32)
    sums = jnp.zeros((1, SIDE), F32)
    row_lse = []
    for k in range(STEPS):
        if k == STEPS // 2:
            wait(copies[near:])
            run(out[1:])
        tile = slice(k * TILE, (k + 1) * TILE)
        logits = scale * lax.dot_general(
            image_ref[tile, :], text, (((1,), (1,)), ((), ())), preferred_element_type=F32
        )
        logits_ref[tile, :] = logits
        row_top = jnp.max(logits, axis=1, keepdims=True)
        row_sum = jnp.sum(jnp.exp2(logits - row_top), axis=1, keepdims=True)
        row_lse.append(to_lanes(row_top + jnp.log2(row_sum)))
        new = jnp.maximum(top, jnp.max(logits, axis=0, keepdims=True))
        sums = sums * jnp.exp2(top - new) + jnp.sum(jnp.exp2(logits - new), axis=0, keepdims=True)
        top = new
    col_lse = top + jnp.log2(sums)
    first = core == 0
    for k in range(STEPS):
        part = col_lse[:, k * TILE : (k + 1) * TILE]
        keep_ref[k : k + 1, :] = jnp.where(first, part, row_lse[k])
        give_ref[k : k + 1, :] = jnp.where(first, row_lse[(k + STEPS // 2) % STEPS], part)
    give_ref[STEPS:, :] = jnp.broadcast_to(pairs_ref[:1, :1], (STEPS, TILE))
    wait(out)


def spread_kernel(at_ref, keep_ref, recv_ref, pairs_ref, out_ref):
    keep, recv = keep_ref[...], recv_ref[:STEPS, :]
    top = jnp.maximum(keep, recv)
    both = top + jnp.log2(jnp.exp2(keep - top) + jnp.exp2(recv - top))
    pairs = recv_ref[STEPS:, :] + pairs_ref[:1, :1]
    first = at_ref[2] == 0
    block = jnp.concatenate([jnp.where(first, keep, both), jnp.where(first, recv, pairs)], axis=0)
    for k in range(PEERS):
        out_ref[pl.ds(k * LINES, LINES), :] = block


def join_kernel(at_ref, parts_ref, keep_ref, give_ref):
    parts = parts_ref[...].reshape(PEERS, LINES, TILE)
    half = lax.broadcasted_iota(jnp.int32, parts.shape, 0) // DEEP
    first = at_ref[2] == 0
    used = first | (half == at_ref[4])
    pairs = jnp.sum(jnp.where(used, parts, 0.0)[:, STEPS:, :1], axis=0)[:1]
    parts = jnp.where(used, parts, LOW)
    top = jnp.max(parts, axis=0)
    lse = top + jnp.log2(jnp.sum(jnp.exp2(parts - top[None]), axis=0))
    low = jnp.sum(lse[:STEPS], keepdims=True)
    high = jnp.sum(lse[STEPS:], keepdims=True)
    term = jnp.broadcast_to(jnp.where(first, low + high, low - 2.0 * pairs), (STEPS, TILE))
    keep_ref[:STEPS, :] = lse[:STEPS]
    keep_ref[STEPS:, :] = term
    turned = jnp.concatenate([lse[STEPS // 2 : STEPS], lse[: STEPS // 2]], axis=0)
    give_ref[:STEPS, :] = jnp.where(first, lse[STEPS:], turned)
    give_ref[STEPS:, :] = term


def tag(term, rows=PIECE):
    term = jnp.broadcast_to(term, (rows, 128))
    high = term.astype(BF16).astype(F32)
    middle = (term - high).astype(BF16).astype(F32)
    low = (term - high) - middle
    lane = lax.rem(lax.broadcasted_iota(jnp.int32, (rows, 128), 1), 4)
    return jnp.where(lane == 0, high, jnp.where(lane == 1, middle, low)).astype(BF16)


def place_tag(at_ref, sums_ref):
    lane = lax.broadcasted_iota(jnp.int32, (1, 128), 1)
    mark = tag(sums_ref[STEPS : STEPS + 1, :1], 16).astype(F32)[:1]
    return jnp.where(lane // 4 == at_ref[3], mark, 0.0)


def untag(row, lane=0):
    return (row[:, lane : lane + 1] + row[:, lane + 1 : lane + 2]) + row[:, lane + 2 : lane + 3]


def weights_kernel(
    at_ref, scale_ref, logits_ref, text_ref, keep_ref, recv_ref,
    weights_ref, turned_ref, other_ref, sums_ref,
):
    first = at_ref[2] == 0
    keep, recv = keep_ref[:STEPS, :], recv_ref[:STEPS, :]
    cols = jnp.where(first, keep, recv)
    col_lse = jnp.concatenate([cols[k : k + 1] for k in range(STEPS)], axis=1)
    rows = jnp.where(first, recv, keep)
    sums_ref[:STEPS, :] = jnp.where(first, recv_ref[STEPS:, :128], keep_ref[STEPS:, :128])
    sums_ref[STEPS:, :] = jnp.where(first, keep_ref[STEPS:, :128], recv_ref[STEPS:, :128])
    row_at = lax.broadcasted_iota(jnp.int32, (TILE, 1), 0) - at_ref[3] * PIECE
    col_at = lax.broadcasted_iota(jnp.int32, (1, SIDE), 1) - at_ref[1] * PIECE
    col_at = jnp.where((col_at >= 0) & (col_at < PIECE), col_at, -SIDE)
    text = text_ref[...]
    for k in (2, 3, 0, 1):
        tile = slice(k * TILE, (k + 1) * TILE)
        logits = logits_ref[tile, :]
        weights = jnp.exp2(logits - to_rows(rows[k : k + 1])) + jnp.exp2(logits - col_lse)
        if k < STEPS // 2:
            weights -= jnp.where(row_at + k * TILE == col_at, 2.0, 0.0)
        weights = (weights * 0.5).astype(BF16)
        turned_ref[:, tile] = weights.T
        if k < STEPS // 2:
            weights_ref[tile, :] = weights
        else:
            other_ref[(k - 2) * TILE : (k - 1) * TILE, :] = (
                scale_ref[0] * jnp.dot(weights, text, preferred_element_type=F32)
            ).astype(BF16)


def text_back_kernel(scale_ref, weights_ref, turned_ref, image_ref, text_ref, sums_ref, out_ref, mine_ref, back, sem):
    image = image_ref[...]
    mark = tag(sums_ref[:1, :1], MARK)
    half = PEERS // 2
    copies = []
    for h in range(2):
        term = (
            scale_ref[0]
            * jnp.dot(turned_ref[h * half * PIECE : (h + 1) * half * PIECE, :], image, preferred_element_type=F32)
        ).astype(BF16)
        for p in range(half):
            start = (h * half + p) * PART
            for b in range(WIDTH // 128):
                back[start + b * PIECE : start + (b + 1) * PIECE, :] = (
                    term[p * PIECE : (p + 1) * PIECE, b * 128 : (b + 1) * 128]
                )
            back[start + PART - MARK : start + PART, :] = mark
        span = pl.ds(h * half * PART, half * PART)
        copies += run([pltpu.make_async_copy(back.at[span, :], out_ref.at[span, :], sem.at[h])])
    mine_ref[...] = scale_ref[0] * jnp.dot(weights_ref[...], text_ref[...], preferred_element_type=F32)
    wait(copies)


HALF = PIECE // 2
FIRST = HALF * (WIDTH // 128) + MARK
AWAY = (3, 2, 1, -3, -2, -1)


def pieces_kernel(at_ref, sums_ref, mine_ref, swapped_ref, begun_ref, out_ref, *refs):
    own_out, up_out, down_out, *away_refs, mine, parts, ends, sem = refs
    mine[...] = mine_ref[...] + swapped_ref[...].astype(F32)

    def block(by):
        return pl.ds(pl.multiple_of(lax.rem(at_ref[3] + by + DEEP, DEEP) * PIECE, PIECE), PIECE)

    across = mine[block(4), :].astype(BF16)
    mark = jnp.broadcast_to(place_tag(at_ref, sums_ref), (MARK, 128)).astype(BF16)
    for h in range(2):
        for b in range(WIDTH // 128):
            ends[h, b * HALF : (b + 1) * HALF, :] = across[h * HALF : (h + 1) * HALF, b * 128 : (b + 1) * 128]
        ends[h, FIRST - MARK :, :] = mark
    copies = run([
        pltpu.make_async_copy(ends.at[0], up_out, sem.at[0]),
        pltpu.make_async_copy(ends.at[1], down_out, sem.at[1]),
        pltpu.make_async_copy(mine.at[block(0), :], own_out, sem.at[2]),
    ])
    for k, (by, ref) in enumerate(zip(AWAY, away_refs)):
        parts[k] = mine[block(by), :].astype(BF16)
        copies += run([pltpu.make_async_copy(parts.at[k], ref, sem.at[3 + k])])
    wait(copies)


def relay_kernel(
    at_ref, sums_ref, up_ref, down_ref, below_ref, above_ref, up_out, down_out, up, down, sem
):
    copies = run([pltpu.make_async_copy(up_ref, up, sem.at[0]), pltpu.make_async_copy(down_ref, down, sem.at[1])])
    mark = place_tag(at_ref, sums_ref)
    for k, (copy, ours, theirs, out) in enumerate(
        zip(copies, (up, down), (below_ref, above_ref), (up_out, down_out))
    ):
        size = theirs.shape[0]
        rows = (size - MARK) // (WIDTH // 128)
        marks = theirs[size - MARK :, :].astype(F32)[:1] + mark
        out[PART - MARK :, :] = jnp.broadcast_to(marks, (MARK, 128)).astype(BF16)
        copy.wait()
        for b in range(WIDTH // 128):
            block = ours[:, b * 128 : (b + 1) * 128].astype(F32)
            came = theirs[b * rows : (b + 1) * rows, :].astype(F32)
            if rows < PIECE:
                rest = jnp.zeros_like(came)
                came = jnp.concatenate([came, rest] if k == 0 else [rest, came], axis=0)
            out[b * PIECE : (b + 1) * PIECE, :] = (block + came).astype(BF16)


def project(back, raw):
    direction, norm = unit_rows(raw)
    along = jnp.sum(direction * back, axis=1, keepdims=True)
    return ((back - direction * along) / norm).astype(BF16)


def text_grad_kernel(raw_ref, loss_ref, parts_ref, out_ref, total_ref, raw, grad, sem):
    copies = run([pltpu.make_async_copy(raw_ref, raw, sem.at[0])])
    total = loss_ref[:1, :1]
    for k in range(PEERS):
        total += untag(parts_ref[(k + 1) * PART - MARK : (k + 1) * PART, :].astype(F32)[:1])
    total_ref[0] = (total * (LN2 / (2.0 * SIDE * PEERS)))[0, 0]
    columns = []
    for b in range(WIDTH // 128):
        column = jnp.zeros((PIECE, 128), F32)
        for k in range(PEERS):
            start = k * PART + b * PIECE
            column += parts_ref[start : start + PIECE, :].astype(F32)
        columns.append(column)
    wait(copies)
    grad[...] = project(jnp.concatenate(columns, axis=1), raw[...])
    wait(run([pltpu.make_async_copy(grad, out_ref, sem.at[0])]))


def image_grad_kernel(at_ref, sums_ref, raw_ref, own_ref, below_ref, above_ref, out_ref, loss_ref, raw, own, grad, sem):
    copies = run([
        pltpu.make_async_copy(raw_ref, raw, sem.at[0]), pltpu.make_async_copy(own_ref, own, sem.at[1])
    ])
    twice = lax.rem(at_ref[3] + DEEP // 2, DEEP)
    lane = lax.broadcasted_iota(jnp.int32, (1, 128), 1)
    marks = place_tag(at_ref, sums_ref) + below_ref[PART - MARK :, :].astype(F32)[:1]
    marks += jnp.where(lane // 4 == twice, 0.0, above_ref[PART - MARK :, :].astype(F32)[:1])
    total = jnp.zeros((1, 1), F32)
    for k in range(DEEP):
        total += untag(marks, 4 * k)
    loss_ref[...] = jnp.broadcast_to(total, loss_ref.shape)
    wait(copies)
    came = [
        below_ref[b * PIECE : (b + 1) * PIECE, :].astype(F32) + above_ref[b * PIECE : (b + 1) * PIECE, :].astype(F32)
        for b in range(WIDTH // 128)
    ]
    back = own[...] + jnp.concatenate(came, axis=1)
    grad[...] = project(back, raw[...])
    wait(run([pltpu.make_async_copy(grad, out_ref, sem.at[0])]))


def gather_image(unit):
    plan, arrays = [(0, 0, 0, PIECE)], [unit]
    up, down, half = unit, unit, PIECE // 2
    for by in range(1, DEEP // 2):
        up, down = send(up, "z", 1), send(down, "z", -1)
        plan += [(0, -by, 0, PIECE), (0, by, 0, PIECE)]
        arrays += [up, down]
    plan += [(0, -(DEEP // 2), 0, half), (0, DEEP // 2, half, half)]
    arrays += [send(up[:half], "z", 1), send(down[half:], "z", -1)]
    plan += [(1, *rest) for _, *rest in plan]
    arrays += [send(a, "c", 1) for a in arrays]
    return plan, arrays


def body(image_emb, text_emb, log_scale):
    width = image_emb.shape[1]
    scale = jnp.exp(log_scale)
    me = lax.axis_index("d")
    z, core, x = me % 8, (me // 8) % 2, me // 64
    at = jnp.stack([me % 16, me // 16, core, z, x % 2]).astype(jnp.int32)
    piece = local((PIECE, width), BF16)
    side = local((SIDE, width), BF16)
    outside = array((SIDE, width), BF16)
    raw = pltpu.VMEM((PIECE, width), BF16)
    sems = pltpu.SemaphoreType.DMA

    image_unit, pairs = call(
        image_unit_kernel, [array((PIECE, width), BF16), local((8, 128), F32)],
        scale, Outside(image_emb), Outside(text_emb), scratch=[raw, raw, raw, sems((3,))],
    )
    plan, pieces = gather_image(image_unit)
    text_units = call(text_units_kernel, outside, Outside(text_emb), scratch=[raw, raw, sems((PEERS,))])
    text = exchange(text_units, XY)


    lines = local((STEPS, TILE), F32)
    image, logits, keep, give = call(
        functools.partial(logits_kernel, plan), [outside, local((SIDE, SIDE), F32), lines, local((2 * STEPS, TILE), F32)],
        at, scale, pairs, text, *map(Outside, pieces),
        scratch=[pltpu.VMEM((SIDE, width), BF16), sems((len(plan),)), sems((2,))],
    )
    spread = call(spread_kernel, local((PEERS * LINES, TILE), F32), at, keep, send(give, "c", 1), pairs)
    lines = local((2 * STEPS, TILE), F32)
    keep, give = call(join_kernel, [lines, lines], at, exchange(spread, MIXED))
    recv = send(give, "c", 1)

    half = (SIDE // 2, width)
    weights, turned, other, sums = call(
        weights_kernel,
        [local((SIDE // 2, SIDE), BF16), local((SIDE, SIDE), BF16), local(half, BF16), local((2 * STEPS, 128), F32)],
        at, scale, logits, text, keep, recv,
    )
    swapped = send(other, "c", 1)
    parts = array((PEERS * PART, 128), BF16)
    text_parts, mine = call(
        text_back_kernel, [parts, local(half, F32)], scale, weights, turned, image, text, sums,
        scratch=[pltpu.VMEM(parts.shape, BF16), sems((2,))],
    )
    end = array((FIRST, 128), BF16)
    away = [array((PIECE, width), BF16)] * len(AWAY)
    text_parts, own, up, down, *away = call(
        pieces_kernel, [parts, array((PIECE, width), F32), end, end, *away],
        at, sums, mine, swapped, Outside(text_parts),
        scratch=[
            pltpu.VMEM(half, F32),
            pltpu.VMEM((len(AWAY), PIECE, width), BF16),
            pltpu.VMEM((2, FIRST, 128), BF16),
            sems((3 + len(AWAY),)),
        ],
        aliases={4: 0},
    )
    text_back = exchange(text_parts, XY)
    below, above = send(up, "z", 1), send(down, "z", -1)
    whole = local((PART, 128), BF16)
    for k in range(3):
        up, down = call(
            relay_kernel, [whole] * 2, at, sums, Outside(away[k]), Outside(away[k + 3]), below, above,
            scratch=[raw, raw, sems((2,))],
        )
        below, above = send(up, "z", 1), send(down, "z", -1)

    grad = array((PIECE, width), BF16)
    grad_image, part = call(
        image_grad_kernel, [grad, local((8, 128), F32)],
        at, sums, Outside(image_emb), Outside(own), below, above,
        scratch=[raw, pltpu.VMEM((PIECE, width), F32), raw, sems((2,))],
    )
    grad_text, loss = call(
        text_grad_kernel, [grad, pltpu.SMEM((1,), F32)], Outside(text_emb), part, text_back,
        scratch=[raw, raw, sems((1,))],
    )
    return loss, grad_image, grad_text


def solution(mesh):
    flat = Mesh(mesh.devices.reshape(-1), ("d",))
    return jax.shard_map(
        body,
        mesh=flat,
        in_specs=(P("d", None), P("d", None), P()),
        out_specs=(P(), P("d", None), P("d", None)),
        check_vma=False,
    )
```

```python
import functools
import math
import typing

import jax
import jax.numpy as jnp
import numpy as np
from jax import lax
from jax.experimental import pallas as pl
from jax.experimental.pallas import tpu as pltpu
from jax.sharding import Mesh, PartitionSpec as P

LOG2E = math.log2(math.e)
LN2 = math.log(2.0)
EPS = 1e-06
LOW = -1e30
PARAMS = pltpu.CompilerParams(vmem_limit_bytes=24 * 1024 * 1024)
HBM = pl.BlockSpec(memory_space=pl.ANY)
WHOLE = pl.BlockSpec(memory_space=pltpu.VMEM)
SCALAR = pl.BlockSpec(memory_space=pltpu.SMEM)
F32 = jnp.float32
BF16 = jnp.bfloat16

INDEX = np.arange(256).reshape(4, 4, 2, 8)
AXES = {"x": 0, "y": 1, "c": 2, "z": 3}
XY = INDEX.transpose(2, 3, 0, 1).reshape(16, 16).tolist()
MIXED = INDEX[:, :, 0, :].transpose(2, 0, 1).reshape(8, 16).tolist() + (
    INDEX[:, :, 1, :].reshape(2, 2, 4, 8).transpose(0, 2, 1, 3).reshape(8, 16).tolist()
)
PEERS = 16
PIECE = 64
SIDE = PEERS * PIECE
TILE = 256
STEPS = SIDE // TILE
DEEP = 8
LINES = 2 * STEPS
WIDTH = 1280
MARK = 16
PART = PIECE * (WIDTH // 128) + MARK


def shift(axis, by):
    to = np.roll(INDEX, -by, AXES[axis])
    return [(int(a), int(b)) for a, b in zip(INDEX.ravel(), to.ravel())]


def send(x, axis, by):
    return lax.ppermute(x, "d", shift(axis, by))


def exchange(x, groups):
    return lax.all_to_all(x, "d", 0, 0, axis_index_groups=groups, tiled=True)


def array(shape, dtype):
    return pltpu.HBM(shape, dtype)


def local(shape, dtype):
    return pltpu.VMEM(shape, dtype)


def call(kernel, outputs, *operands, scratch=(), aliases={}):
    specs, arrays = [], []
    for x in operands:
        if isinstance(x, Outside):
            specs.append(HBM)
            arrays.append(pltpu.with_memory_space_constraint(x.array, pltpu.HBM))
        elif x.size <= 8:
            specs.append(SCALAR)
            arrays.append(x)
        else:
            specs.append(WHOLE)
            arrays.append(pltpu.with_memory_space_constraint(x, pltpu.VMEM))
    return pl.pallas_call(
        kernel,
        out_shape=outputs,
        in_specs=specs,
        out_specs=jax.tree.map(lambda s: {pltpu.VMEM: WHOLE, pltpu.SMEM: SCALAR}.get(s.memory_space, HBM), outputs),
        scratch_shapes=list(scratch),
        input_output_aliases=aliases,
        compiler_params=PARAMS,
    )(*arrays)


class Outside(typing.NamedTuple):
    array: typing.Any


def run(copies):
    for copy in copies:
        copy.start()
    return copies


def wait(copies):
    for copy in copies:
        copy.wait()


def unit_rows(raw):
    values = raw.astype(F32)
    norm = jnp.sqrt(jnp.sum(values * values, axis=1, keepdims=True) + EPS)
    return values / norm, norm


def image_unit_kernel(scale_ref, raw_ref, text_ref, out_ref, pairs_ref, raw, text, unit, sem):
    copies = run([
        pltpu.make_async_copy(raw_ref, raw, sem.at[0]), pltpu.make_async_copy(text_ref, text, sem.at[1])
    ])
    copies[0].wait()
    unit[...] = unit_rows(raw[...])[0].astype(BF16)
    out = run([pltpu.make_async_copy(unit, out_ref, sem.at[2])])
    copies[1].wait()
    other = unit_rows(text[...])[0].astype(BF16)
    total = jnp.sum(unit[...].astype(F32) * other.astype(F32), keepdims=True)
    pairs_ref[...] = jnp.broadcast_to(total * (scale_ref[0] * LOG2E), pairs_ref.shape)
    wait(out)


def text_units_kernel(raw_ref, out_ref, raw, unit, sem):
    wait(run([pltpu.make_async_copy(raw_ref, raw, sem.at[0])]))
    unit[...] = unit_rows(raw[...])[0].astype(BF16)
    wait(run([
        pltpu.make_async_copy(unit, out_ref.at[pl.ds(k * PIECE, PIECE), :], sem.at[k])
        for k in range(PEERS)
    ]))


def to_lanes(column):
    return jnp.broadcast_to(column, (column.shape[0], 128)).T[:1, :]


def to_rows(lanes):
    return jnp.broadcast_to(lanes, (128, lanes.shape[1])).T[:, :1]


def logits_kernel(plan, at_ref, scale_ref, pairs_ref, text_ref, *refs):
    pieces = refs[: len(plan)]
    image_out, logits_ref, keep_ref, give_ref, image_ref, sem, out_sem = refs[len(plan) :]
    core = at_ref[2]
    copies = []
    for k, (piece, (flip, by, start, rows)) in enumerate(zip(pieces, plan)):
        block = lax.rem(at_ref[3] + by + DEEP, DEEP)
        first = pl.multiple_of(flip * (SIDE // 2) + block * PIECE + start, 32)
        copies.append(pltpu.make_async_copy(piece, image_ref.at[pl.ds(first, rows), :], sem.at[k]))
    near = len(plan) // 2
    halves = [pl.ds(k * (SIDE // 2), SIDE // 2) for k in range(2)]
    out = [pltpu.make_async_copy(image_ref.at[h, :], image_out.at[h, :], out_sem.at[k]) for k, h in enumerate(halves)]
    wait(run(copies[:near]))
    run(copies[near:] + out[:1])
    text = text_ref[...]
    scale = scale_ref[0] * LOG2E
    top = jnp.full((1, SIDE), LOW, F32)
    sums = jnp.zeros((1, SIDE), F32)
    row_lse = []
    for k in range(STEPS):
        if k == STEPS // 2:
            wait(copies[near:])
            run(out[1:])
        tile = slice(k * TILE, (k + 1) * TILE)
        logits = scale * lax.dot_general(
            image_ref[tile, :], text, (((1,), (1,)), ((), ())), preferred_element_type=F32
        )
        logits_ref[tile, :] = logits
        row_top = jnp.max(logits, axis=1, keepdims=True)
        row_sum = jnp.sum(jnp.exp2(logits - row_top), axis=1, keepdims=True)
        row_lse.append(to_lanes(row_top + jnp.log2(row_sum)))
        new = jnp.maximum(top, jnp.max(logits, axis=0, keepdims=True))
        sums = sums * jnp.exp2(top - new) + jnp.sum(jnp.exp2(logits - new), axis=0, keepdims=True)
        top = new
    col_lse = top + jnp.log2(sums)
    first = core == 0
    for k in range(STEPS):
        part = col_lse[:, k * TILE : (k + 1) * TILE]
        keep_ref[k : k + 1, :] = jnp.where(first, part, row_lse[k])
        give_ref[k : k + 1, :] = jnp.where(first, row_lse[(k + STEPS // 2) % STEPS], part)
    give_ref[STEPS:, :] = jnp.broadcast_to(pairs_ref[:1, :1], (STEPS, TILE))
    wait(out)


def spread_kernel(at_ref, keep_ref, recv_ref, pairs_ref, out_ref):
    keep, recv = keep_ref[...], recv_ref[:STEPS, :]
    top = jnp.maximum(keep, recv)
    both = top + jnp.log2(jnp.exp2(keep - top) + jnp.exp2(recv - top))
    pairs = recv_ref[STEPS:, :] + pairs_ref[:1, :1]
    first = at_ref[2] == 0
    block = jnp.concatenate([jnp.where(first, keep, both), jnp.where(first, recv, pairs)], axis=0)
    for k in range(PEERS):
        out_ref[pl.ds(k * LINES, LINES), :] = block


def join_kernel(at_ref, parts_ref, keep_ref, give_ref):
    parts = parts_ref[...].reshape(PEERS, LINES, TILE)
    half = lax.broadcasted_iota(jnp.int32, parts.shape, 0) // DEEP
    first = at_ref[2] == 0
    used = first | (half == at_ref[4])
    pairs = jnp.sum(jnp.where(used, parts, 0.0)[:, STEPS:, :1], axis=0)[:1]
    parts = jnp.where(used, parts, LOW)
    top = jnp.max(parts, axis=0)
    lse = top + jnp.log2(jnp.sum(jnp.exp2(parts - top[None]), axis=0))
    low = jnp.sum(lse[:STEPS], keepdims=True)
    high = jnp.sum(lse[STEPS:], keepdims=True)
    term = jnp.broadcast_to(jnp.where(first, low + high, low - 2.0 * pairs), (STEPS, TILE))
    keep_ref[:STEPS, :] = lse[:STEPS]
    keep_ref[STEPS:, :] = term
    turned = jnp.concatenate([lse[STEPS // 2 : STEPS], lse[: STEPS // 2]], axis=0)
    give_ref[:STEPS, :] = jnp.where(first, lse[STEPS:], turned)
    give_ref[STEPS:, :] = term


def tag(term, rows=PIECE):
    term = jnp.broadcast_to(term, (rows, 128))
    high = term.astype(BF16).astype(F32)
    middle = (term - high).astype(BF16).astype(F32)
    low = (term - high) - middle
    lane = lax.rem(lax.broadcasted_iota(jnp.int32, (rows, 128), 1), 4)
    return jnp.where(lane == 0, high, jnp.where(lane == 1, middle, low)).astype(BF16)


def place_tag(at_ref, sums_ref):
    lane = lax.broadcasted_iota(jnp.int32, (1, 128), 1)
    mark = tag(sums_ref[STEPS : STEPS + 1, :1], 16).astype(F32)[:1]
    return jnp.where(lane // 4 == at_ref[3], mark, 0.0)


def untag(row, lane=0):
    return (row[:, lane : lane + 1] + row[:, lane + 1 : lane + 2]) + row[:, lane + 2 : lane + 3]


def weights_kernel(
    at_ref, scale_ref, logits_ref, text_ref, keep_ref, recv_ref,
    weights_ref, turned_ref, other_ref, sums_ref,
):
    first = at_ref[2] == 0
    keep, recv = keep_ref[:STEPS, :], recv_ref[:STEPS, :]
    cols = jnp.where(first, keep, recv)
    col_lse = jnp.concatenate([cols[k : k + 1] for k in range(STEPS)], axis=1)
    rows = jnp.where(first, recv, keep)
    sums_ref[:STEPS, :] = jnp.where(first, recv_ref[STEPS:, :128], keep_ref[STEPS:, :128])
    sums_ref[STEPS:, :] = jnp.where(first, keep_ref[STEPS:, :128], recv_ref[STEPS:, :128])
    row_at = lax.broadcasted_iota(jnp.int32, (TILE, 1), 0) - at_ref[3] * PIECE
    col_at = lax.broadcasted_iota(jnp.int32, (1, SIDE), 1) - at_ref[1] * PIECE
    col_at = jnp.where((col_at >= 0) & (col_at < PIECE), col_at, -SIDE)
    text = text_ref[...]
    for k in (2, 3, 0, 1):
        tile = slice(k * TILE, (k + 1) * TILE)
        logits = logits_ref[tile, :]
        weights = jnp.exp2(logits - to_rows(rows[k : k + 1])) + jnp.exp2(logits - col_lse)
        if k < STEPS // 2:
            weights -= jnp.where(row_at + k * TILE == col_at, 2.0, 0.0)
        weights = (weights * 0.5).astype(BF16)
        turned_ref[:, tile] = weights.T
        if k < STEPS // 2:
            weights_ref[tile, :] = weights
        else:
            other_ref[(k - 2) * TILE : (k - 1) * TILE, :] = (
                scale_ref[0] * jnp.dot(weights, text, preferred_element_type=F32)
            ).astype(BF16)


def text_back_kernel(scale_ref, weights_ref, turned_ref, image_ref, text_ref, sums_ref, out_ref, mine_ref, back, sem):
    image = image_ref[...]
    mark = tag(sums_ref[:1, :1], MARK)
    half = PEERS // 2
    copies = []
    for h in range(2):
        term = (
            scale_ref[0]
            * jnp.dot(turned_ref[h * half * PIECE : (h + 1) * half * PIECE, :], image, preferred_element_type=F32)
        ).astype(BF16)
        for p in range(half):
            start = (h * half + p) * PART
            for b in range(WIDTH // 128):
                back[start + b * PIECE : start + (b + 1) * PIECE, :] = (
                    term[p * PIECE : (p + 1) * PIECE, b * 128 : (b + 1) * 128]
                )
            back[start + PART - MARK : start + PART, :] = mark
        span = pl.ds(h * half * PART, half * PART)
        copies += run([pltpu.make_async_copy(back.at[span, :], out_ref.at[span, :], sem.at[h])])
    mine_ref[...] = scale_ref[0] * jnp.dot(weights_ref[...], text_ref[...], preferred_element_type=F32)
    wait(copies)


HALF = PIECE // 2
FIRST = HALF * (WIDTH // 128) + MARK
AWAY = (3, 2, 1, -3, -2, -1)


def pieces_kernel(at_ref, sums_ref, mine_ref, swapped_ref, begun_ref, out_ref, *refs):
    own_out, up_out, down_out, *away_refs, own, parts, ends, sem = refs

    def block(by):
        rows = pl.ds(pl.multiple_of(lax.rem(at_ref[3] + by + DEEP, DEEP) * PIECE, PIECE), PIECE)
        return mine_ref[rows, :] + swapped_ref[rows, :].astype(F32)

    copies = []
    for k, (by, ref) in enumerate(zip(AWAY, away_refs)):
        parts[k] = block(by).astype(BF16)
        copies += run([pltpu.make_async_copy(parts.at[k], ref, sem.at[3 + k])])
    own[...] = block(0)
    copies += run([pltpu.make_async_copy(own, own_out, sem.at[2])])
    across = block(4).astype(BF16)
    mark = jnp.broadcast_to(place_tag(at_ref, sums_ref), (MARK, 128)).astype(BF16)
    for h, out in enumerate((up_out, down_out)):
        for b in range(WIDTH // 128):
            ends[h, b * HALF : (b + 1) * HALF, :] = across[h * HALF : (h + 1) * HALF, b * 128 : (b + 1) * 128]
        ends[h, FIRST - MARK :, :] = mark
        copies += run([pltpu.make_async_copy(ends.at[h], out, sem.at[h])])
    wait(copies)


def relay_kernel(
    at_ref, sums_ref, up_ref, down_ref, below_ref, above_ref, up_out, down_out, up, down, sem
):
    copies = run([pltpu.make_async_copy(up_ref, up, sem.at[0]), pltpu.make_async_copy(down_ref, down, sem.at[1])])
    mark = place_tag(at_ref, sums_ref)
    for k, (copy, ours, theirs, out) in enumerate(
        zip(copies, (up, down), (below_ref, above_ref), (up_out, down_out))
    ):
        size = theirs.shape[0]
        rows = (size - MARK) // (WIDTH // 128)
        marks = theirs[size - MARK :, :].astype(F32)[:1] + mark
        out[PART - MARK :, :] = jnp.broadcast_to(marks, (MARK, 128)).astype(BF16)
        copy.wait()
        for b in range(WIDTH // 128):
            block = ours[:, b * 128 : (b + 1) * 128].astype(F32)
            came = theirs[b * rows : (b + 1) * rows, :].astype(F32)
            if rows < PIECE:
                rest = jnp.zeros_like(came)
                came = jnp.concatenate([came, rest] if k == 0 else [rest, came], axis=0)
            out[b * PIECE : (b + 1) * PIECE, :] = (block + came).astype(BF16)


def project(back, raw):
    direction, norm = unit_rows(raw)
    along = jnp.sum(direction * back, axis=1, keepdims=True)
    return ((back - direction * along) / norm).astype(BF16)


def text_grad_kernel(raw_ref, loss_ref, parts_ref, out_ref, total_ref, raw, grad, sem):
    copies = run([pltpu.make_async_copy(raw_ref, raw, sem.at[0])])
    total = loss_ref[:1, :1]
    for k in range(PEERS):
        total += untag(parts_ref[(k + 1) * PART - MARK : (k + 1) * PART, :].astype(F32)[:1])
    total_ref[0] = (total * (LN2 / (2.0 * SIDE * PEERS)))[0, 0]
    columns = []
    for b in range(WIDTH // 128):
        column = jnp.zeros((PIECE, 128), F32)
        for k in range(PEERS):
            start = k * PART + b * PIECE
            column += parts_ref[start : start + PIECE, :].astype(F32)
        columns.append(column)
    wait(copies)
    grad[...] = project(jnp.concatenate(columns, axis=1), raw[...])
    wait(run([pltpu.make_async_copy(grad, out_ref, sem.at[0])]))


def image_grad_kernel(at_ref, sums_ref, raw_ref, own_ref, below_ref, above_ref, out_ref, loss_ref, raw, own, grad, sem):
    copies = run([
        pltpu.make_async_copy(raw_ref, raw, sem.at[0]), pltpu.make_async_copy(own_ref, own, sem.at[1])
    ])
    twice = lax.rem(at_ref[3] + DEEP // 2, DEEP)
    lane = lax.broadcasted_iota(jnp.int32, (1, 128), 1)
    marks = place_tag(at_ref, sums_ref) + below_ref[PART - MARK :, :].astype(F32)[:1]
    marks += jnp.where(lane // 4 == twice, 0.0, above_ref[PART - MARK :, :].astype(F32)[:1])
    total = jnp.zeros((1, 1), F32)
    for k in range(DEEP):
        total += untag(marks, 4 * k)
    loss_ref[...] = jnp.broadcast_to(total, loss_ref.shape)
    wait(copies)
    came = [
        below_ref[b * PIECE : (b + 1) * PIECE, :].astype(F32) + above_ref[b * PIECE : (b + 1) * PIECE, :].astype(F32)
        for b in range(WIDTH // 128)
    ]
    back = own[...] + jnp.concatenate(came, axis=1)
    grad[...] = project(back, raw[...])
    wait(run([pltpu.make_async_copy(grad, out_ref, sem.at[0])]))


def gather_image(unit):
    plan, arrays = [(0, 0, 0, PIECE)], [unit]
    up, down, half = unit, unit, PIECE // 2
    for by in range(1, DEEP // 2):
        up, down = send(up, "z", 1), send(down, "z", -1)
        plan += [(0, -by, 0, PIECE), (0, by, 0, PIECE)]
        arrays += [up, down]
    plan += [(0, -(DEEP // 2), 0, half), (0, DEEP // 2, half, half)]
    arrays += [send(up[:half], "z", 1), send(down[half:], "z", -1)]
    plan += [(1, *rest) for _, *rest in plan]
    arrays += [send(a, "c", 1) for a in arrays]
    return plan, arrays


def body(image_emb, text_emb, log_scale):
    width = image_emb.shape[1]
    scale = jnp.exp(log_scale)
    me = lax.axis_index("d")
    z, core, x = me % 8, (me // 8) % 2, me // 64
    at = jnp.stack([me % 16, me // 16, core, z, x % 2]).astype(jnp.int32)
    piece = local((PIECE, width), BF16)
    side = local((SIDE, width), BF16)
    outside = array((SIDE, width), BF16)
    raw = pltpu.VMEM((PIECE, width), BF16)
    sems = pltpu.SemaphoreType.DMA

    image_unit, pairs = call(
        image_unit_kernel, [array((PIECE, width), BF16), local((8, 128), F32)],
        scale, Outside(image_emb), Outside(text_emb), scratch=[raw, raw, raw, sems((3,))],
    )
    plan, pieces = gather_image(image_unit)
    text_units = call(text_units_kernel, outside, Outside(text_emb), scratch=[raw, raw, sems((PEERS,))])
    text = exchange(text_units, XY)


    lines = local((STEPS, TILE), F32)
    image, logits, keep, give = call(
        functools.partial(logits_kernel, plan), [outside, local((SIDE, SIDE), F32), lines, local((2 * STEPS, TILE), F32)],
        at, scale, pairs, text, *map(Outside, pieces),
        scratch=[pltpu.VMEM((SIDE, width), BF16), sems((len(plan),)), sems((2,))],
    )
    spread = call(spread_kernel, local((PEERS * LINES, TILE), F32), at, keep, send(give, "c", 1), pairs)
    lines = local((2 * STEPS, TILE), F32)
    keep, give = call(join_kernel, [lines, lines], at, exchange(spread, MIXED))
    recv = send(give, "c", 1)

    half = (SIDE // 2, width)
    weights, turned, other, sums = call(
        weights_kernel,
        [local((SIDE // 2, SIDE), BF16), local((SIDE, SIDE), BF16), local(half, BF16), local((2 * STEPS, 128), F32)],
        at, scale, logits, text, keep, recv,
    )
    swapped = send(other, "c", 1)
    parts = array((PEERS * PART, 128), BF16)
    text_parts, mine = call(
        text_back_kernel, [parts, local(half, F32)], scale, weights, turned, image, text, sums,
        scratch=[pltpu.VMEM(parts.shape, BF16), sems((2,))],
    )
    end = array((FIRST, 128), BF16)
    away = [array((PIECE, width), BF16)] * len(AWAY)
    text_parts, own, up, down, *away = call(
        pieces_kernel, [parts, array((PIECE, width), F32), end, end, *away],
        at, sums, mine, swapped, Outside(text_parts),
        scratch=[
            pltpu.VMEM((PIECE, width), F32),
            pltpu.VMEM((len(AWAY), PIECE, width), BF16),
            pltpu.VMEM((2, FIRST, 128), BF16),
            sems((3 + len(AWAY),)),
        ],
        aliases={4: 0},
    )
    text_back = exchange(text_parts, XY)
    below, above = send(up, "z", 1), send(down, "z", -1)
    whole = local((PART, 128), BF16)
    for k in range(3):
        up, down = call(
            relay_kernel, [whole] * 2, at, sums, Outside(away[k]), Outside(away[k + 3]), below, above,
            scratch=[raw, raw, sems((2,))],
        )
        below, above = send(up, "z", 1), send(down, "z", -1)

    grad = array((PIECE, width), BF16)
    grad_image, part = call(
        image_grad_kernel, [grad, local((8, 128), F32)],
        at, sums, Outside(image_emb), Outside(own), below, above,
        scratch=[raw, pltpu.VMEM((PIECE, width), F32), raw, sems((2,))],
    )
    grad_text, loss = call(
        text_grad_kernel, [grad, pltpu.SMEM((1,), F32)], Outside(text_emb), part, text_back,
        scratch=[raw, raw, sems((1,))],
    )
    return loss, grad_image, grad_text


def solution(mesh):
    flat = Mesh(mesh.devices.reshape(-1), ("d",))
    return jax.shard_map(
        body,
        mesh=flat,
        in_specs=(P("d", None), P("d", None), P()),
        out_specs=(P(), P("d", None), P("d", None)),
        check_vma=False,
    )
```

```python
import functools
import math
import typing

import jax
import jax.numpy as jnp
import numpy as np
from jax import lax
from jax.experimental import pallas as pl
from jax.experimental.pallas import tpu as pltpu
from jax.sharding import Mesh, PartitionSpec as P

LOG2E = math.log2(math.e)
LN2 = math.log(2.0)
EPS = 1e-06
LOW = -1e30
PARAMS = pltpu.CompilerParams(vmem_limit_bytes=24 * 1024 * 1024)
HBM = pl.BlockSpec(memory_space=pl.ANY)
WHOLE = pl.BlockSpec(memory_space=pltpu.VMEM)
SCALAR = pl.BlockSpec(memory_space=pltpu.SMEM)
F32 = jnp.float32
BF16 = jnp.bfloat16

INDEX = np.arange(256).reshape(4, 4, 2, 8)
AXES = {"x": 0, "y": 1, "c": 2, "z": 3}
XY = INDEX.transpose(2, 3, 0, 1).reshape(16, 16).tolist()
MIXED = INDEX[:, :, 0, :].transpose(2, 0, 1).reshape(8, 16).tolist() + (
    INDEX[:, :, 1, :].reshape(2, 2, 4, 8).transpose(0, 2, 1, 3).reshape(8, 16).tolist()
)
PEERS = 16
PIECE = 64
SIDE = PEERS * PIECE
TILE = 256
STEPS = SIDE // TILE
DEEP = 8
LINES = 2 * STEPS
WIDTH = 1280
MARK = 16
PART = PIECE * (WIDTH // 128) + MARK


def shift(axis, by):
    to = np.roll(INDEX, -by, AXES[axis])
    return [(int(a), int(b)) for a, b in zip(INDEX.ravel(), to.ravel())]


def send(x, axis, by):
    return lax.ppermute(x, "d", shift(axis, by))


def exchange(x, groups):
    return lax.all_to_all(x, "d", 0, 0, axis_index_groups=groups, tiled=True)


def array(shape, dtype):
    return pltpu.HBM(shape, dtype)


def local(shape, dtype):
    return pltpu.VMEM(shape, dtype)


def call(kernel, outputs, *operands, scratch=(), aliases={}):
    specs, arrays = [], []
    for x in operands:
        if isinstance(x, Outside):
            specs.append(HBM)
            arrays.append(pltpu.with_memory_space_constraint(x.array, pltpu.HBM))
        elif x.size <= 8:
            specs.append(SCALAR)
            arrays.append(x)
        else:
            specs.append(WHOLE)
            arrays.append(pltpu.with_memory_space_constraint(x, pltpu.VMEM))
    return pl.pallas_call(
        kernel,
        out_shape=outputs,
        in_specs=specs,
        out_specs=jax.tree.map(lambda s: {pltpu.VMEM: WHOLE, pltpu.SMEM: SCALAR}.get(s.memory_space, HBM), outputs),
        scratch_shapes=list(scratch),
        input_output_aliases=aliases,
        compiler_params=PARAMS,
    )(*arrays)


class Outside(typing.NamedTuple):
    array: typing.Any


def run(copies):
    for copy in copies:
        copy.start()
    return copies


def wait(copies):
    for copy in copies:
        copy.wait()


def unit_rows(raw):
    values = raw.astype(F32)
    norm = jnp.sqrt(jnp.sum(values * values, axis=1, keepdims=True) + EPS)
    return values / norm, norm


def units_kernel(
    text_ref, image_ref, text_out, image_out, pairs_ref, text_raw, image_raw, text, image, sem, out_sem
):
    copies = run([
        pltpu.make_async_copy(text_ref, text_raw, sem.at[0]), pltpu.make_async_copy(image_ref, image_raw, sem.at[1])
    ])
    copies[0].wait()
    text[...] = unit_rows(text_raw[...])[0].astype(BF16)
    out = run([
        pltpu.make_async_copy(text, text_out.at[pl.ds(k * PIECE, PIECE), :], out_sem.at[k]) for k in range(PEERS)
    ])
    copies[1].wait()
    image[...] = unit_rows(image_raw[...])[0].astype(BF16)
    out += run([pltpu.make_async_copy(image, image_out, out_sem.at[PEERS])])
    total = jnp.sum(image[...].astype(F32) * text[...].astype(F32), keepdims=True)
    pairs_ref[...] = jnp.broadcast_to(total, pairs_ref.shape)
    wait(out)


def to_lanes(column):
    return jnp.broadcast_to(column, (column.shape[0], 128)).T[:1, :]


def to_rows(lanes):
    return jnp.broadcast_to(lanes, (128, lanes.shape[1])).T[:, :1]


def logits_kernel(plan, at_ref, scale_ref, pairs_ref, text_ref, *refs):
    pieces = refs[: len(plan)]
    image_out, logits_ref, keep_ref, give_ref, image_ref, sem, out_sem = refs[len(plan) :]
    core = at_ref[2]
    copies = []
    for k, (piece, (flip, by, start, rows)) in enumerate(zip(pieces, plan)):
        block = lax.rem(at_ref[3] + by + DEEP, DEEP)
        first = pl.multiple_of(flip * (SIDE // 2) + block * PIECE + start, 32)
        copies.append(pltpu.make_async_copy(piece, image_ref.at[pl.ds(first, rows), :], sem.at[k]))
    near = len(plan) // 2
    halves = [pl.ds(k * (SIDE // 2), SIDE // 2) for k in range(2)]
    out = [pltpu.make_async_copy(image_ref.at[h, :], image_out.at[h, :], out_sem.at[k]) for k, h in enumerate(halves)]
    wait(run(copies[:near]))
    run(copies[near:] + out[:1])
    text = text_ref[...]
    scale = scale_ref[0] * LOG2E
    top = jnp.full((1, SIDE), LOW, F32)
    sums = jnp.zeros((1, SIDE), F32)
    row_lse = []
    for k in range(STEPS):
        if k == STEPS // 2:
            wait(copies[near:])
            run(out[1:])
        tile = slice(k * TILE, (k + 1) * TILE)
        logits = scale * lax.dot_general(
            image_ref[tile, :], text, (((1,), (1,)), ((), ())), preferred_element_type=F32
        )
        logits_ref[tile, :] = logits
        row_top = jnp.max(logits, axis=1, keepdims=True)
        row_sum = jnp.sum(jnp.exp2(logits - row_top), axis=1, keepdims=True)
        row_lse.append(to_lanes(row_top + jnp.log2(row_sum)))
        new = jnp.maximum(top, jnp.max(logits, axis=0, keepdims=True))
        sums = sums * jnp.exp2(top - new) + jnp.sum(jnp.exp2(logits - new), axis=0, keepdims=True)
        top = new
    col_lse = top + jnp.log2(sums)
    first = core == 0
    for k in range(STEPS):
        part = col_lse[:, k * TILE : (k + 1) * TILE]
        keep_ref[k : k + 1, :] = jnp.where(first, part, row_lse[k])
        give_ref[k : k + 1, :] = jnp.where(first, row_lse[(k + STEPS // 2) % STEPS], part)
    pairs = jnp.broadcast_to(pairs_ref[:1, :1] * scale, (STEPS, TILE))
    keep_ref[STEPS:, :] = pairs
    give_ref[STEPS:, :] = pairs
    wait(out)


def spread_kernel(at_ref, keep_ref, recv_ref, out_ref):
    keep, recv = keep_ref[:STEPS, :], recv_ref[:STEPS, :]
    top = jnp.maximum(keep, recv)
    both = top + jnp.log2(jnp.exp2(keep - top) + jnp.exp2(recv - top))
    pairs = keep_ref[STEPS:, :] + recv_ref[STEPS:, :]
    first = at_ref[2] == 0
    block = jnp.concatenate([jnp.where(first, keep, both), jnp.where(first, recv, pairs)], axis=0)
    for k in range(PEERS):
        out_ref[pl.ds(k * LINES, LINES), :] = block


def join_kernel(at_ref, parts_ref, keep_ref, give_ref):
    parts = parts_ref[...].reshape(PEERS, LINES, TILE)
    half = lax.broadcasted_iota(jnp.int32, parts.shape, 0) // DEEP
    first = at_ref[2] == 0
    used = first | (half == at_ref[4])
    pairs = jnp.sum(jnp.where(used, parts, 0.0)[:, STEPS:, :1], axis=0)[:1]
    parts = jnp.where(used, parts, LOW)
    top = jnp.max(parts, axis=0)
    lse = top + jnp.log2(jnp.sum(jnp.exp2(parts - top[None]), axis=0))
    low = jnp.sum(lse[:STEPS], keepdims=True)
    high = jnp.sum(lse[STEPS:], keepdims=True)
    term = jnp.broadcast_to(jnp.where(first, low + high, low - 2.0 * pairs), (STEPS, TILE))
    keep_ref[:STEPS, :] = lse[:STEPS]
    keep_ref[STEPS:, :] = term
    turned = jnp.concatenate([lse[STEPS // 2 : STEPS], lse[: STEPS // 2]], axis=0)
    give_ref[:STEPS, :] = jnp.where(first, lse[STEPS:], turned)
    give_ref[STEPS:, :] = term


def tag(term, rows=PIECE):
    term = jnp.broadcast_to(term, (rows, 128))
    high = term.astype(BF16).astype(F32)
    middle = (term - high).astype(BF16).astype(F32)
    low = (term - high) - middle
    lane = lax.rem(lax.broadcasted_iota(jnp.int32, (rows, 128), 1), 4)
    return jnp.where(lane == 0, high, jnp.where(lane == 1, middle, low)).astype(BF16)


def place_tag(at_ref, sums_ref):
    lane = lax.broadcasted_iota(jnp.int32, (1, 128), 1)
    mark = tag(sums_ref[STEPS : STEPS + 1, :1], 16).astype(F32)[:1]
    return jnp.where(lane // 4 == at_ref[3], mark, 0.0)


def untag(row, lane=0):
    return (row[:, lane : lane + 1] + row[:, lane + 1 : lane + 2]) + row[:, lane + 2 : lane + 3]


def weights_kernel(
    at_ref, scale_ref, logits_ref, text_ref, keep_ref, recv_ref,
    weights_ref, turned_ref, other_ref, sums_ref,
):
    first = at_ref[2] == 0
    keep, recv = keep_ref[:STEPS, :], recv_ref[:STEPS, :]
    cols = jnp.where(first, keep, recv)
    col_lse = jnp.concatenate([cols[k : k + 1] for k in range(STEPS)], axis=1)
    rows = jnp.where(first, recv, keep)
    sums_ref[:STEPS, :] = jnp.where(first, recv_ref[STEPS:, :128], keep_ref[STEPS:, :128])
    sums_ref[STEPS:, :] = jnp.where(first, keep_ref[STEPS:, :128], recv_ref[STEPS:, :128])
    row_at = lax.broadcasted_iota(jnp.int32, (TILE, 1), 0) - at_ref[3] * PIECE
    col_at = lax.broadcasted_iota(jnp.int32, (1, SIDE), 1) - at_ref[1] * PIECE
    col_at = jnp.where((col_at >= 0) & (col_at < PIECE), col_at, -SIDE)
    text = text_ref[...]
    for k in (2, 3, 0, 1):
        tile = slice(k * TILE, (k + 1) * TILE)
        logits = logits_ref[tile, :]
        weights = jnp.exp2(logits - to_rows(rows[k : k + 1])) + jnp.exp2(logits - col_lse)
        if k < STEPS // 2:
            weights -= jnp.where(row_at + k * TILE == col_at, 2.0, 0.0)
        weights = (weights * 0.5).astype(BF16)
        turned_ref[:, tile] = weights.T
        if k < STEPS // 2:
            weights_ref[tile, :] = weights
        else:
            other_ref[(k - 2) * TILE : (k - 1) * TILE, :] = (
                scale_ref[0] * jnp.dot(weights, text, preferred_element_type=F32)
            ).astype(BF16)


def text_back_kernel(scale_ref, weights_ref, turned_ref, image_ref, text_ref, sums_ref, out_ref, mine_ref, back, sem):
    image = image_ref[...]
    mark = tag(sums_ref[:1, :1], MARK)
    half = PEERS // 2
    copies = []
    for h in range(2):
        term = (
            scale_ref[0]
            * jnp.dot(turned_ref[h * half * PIECE : (h + 1) * half * PIECE, :], image, preferred_element_type=F32)
        ).astype(BF16)
        for p in range(half):
            start = (h * half + p) * PART
            for b in range(WIDTH // 128):
                back[start + b * PIECE : start + (b + 1) * PIECE, :] = (
                    term[p * PIECE : (p + 1) * PIECE, b * 128 : (b + 1) * 128]
                )
            back[start + PART - MARK : start + PART, :] = mark
        span = pl.ds(h * half * PART, half * PART)
        copies += run([pltpu.make_async_copy(back.at[span, :], out_ref.at[span, :], sem.at[h])])
    mine_ref[...] = scale_ref[0] * jnp.dot(weights_ref[...], text_ref[...], preferred_element_type=F32)
    wait(copies)


HALF = PIECE // 2
FIRST = HALF * (WIDTH // 128) + MARK
AWAY = (3, 2, 1, -3, -2, -1)


def pieces_kernel(at_ref, sums_ref, mine_ref, swapped_ref, begun_ref, out_ref, *refs):
    own_out, up_out, down_out, *away_refs, own, parts, ends, sem = refs

    def block(by):
        rows = pl.ds(pl.multiple_of(lax.rem(at_ref[3] + by + DEEP, DEEP) * PIECE, PIECE), PIECE)
        return mine_ref[rows, :] + swapped_ref[rows, :].astype(F32)

    copies = []
    for k, (by, ref) in enumerate(zip(AWAY, away_refs)):
        parts[k] = block(by).astype(BF16)
        copies += run([pltpu.make_async_copy(parts.at[k], ref, sem.at[3 + k])])
    own[...] = block(0)
    copies += run([pltpu.make_async_copy(own, own_out, sem.at[2])])
    across = block(4).astype(BF16)
    mark = jnp.broadcast_to(place_tag(at_ref, sums_ref), (MARK, 128)).astype(BF16)
    for h, out in enumerate((up_out, down_out)):
        for b in range(WIDTH // 128):
            ends[h, b * HALF : (b + 1) * HALF, :] = across[h * HALF : (h + 1) * HALF, b * 128 : (b + 1) * 128]
        ends[h, FIRST - MARK :, :] = mark
        copies += run([pltpu.make_async_copy(ends.at[h], out, sem.at[h])])
    wait(copies)


def relay_kernel(
    at_ref, sums_ref, up_ref, down_ref, below_ref, above_ref, up_out, down_out, up, down, sem
):
    copies = run([pltpu.make_async_copy(up_ref, up, sem.at[0]), pltpu.make_async_copy(down_ref, down, sem.at[1])])
    mark = place_tag(at_ref, sums_ref)
    for k, (copy, ours, theirs, out) in enumerate(
        zip(copies, (up, down), (below_ref, above_ref), (up_out, down_out))
    ):
        size = theirs.shape[0]
        rows = (size - MARK) // (WIDTH // 128)
        marks = theirs[size - MARK :, :].astype(F32)[:1] + mark
        out[PART - MARK :, :] = jnp.broadcast_to(marks, (MARK, 128)).astype(BF16)
        copy.wait()
        for b in range(WIDTH // 128):
            block = ours[:, b * 128 : (b + 1) * 128].astype(F32)
            came = theirs[b * rows : (b + 1) * rows, :].astype(F32)
            if rows < PIECE:
                rest = jnp.zeros_like(came)
                came = jnp.concatenate([came, rest] if k == 0 else [rest, came], axis=0)
            out[b * PIECE : (b + 1) * PIECE, :] = (block + came).astype(BF16)


def project(back, raw):
    direction, norm = unit_rows(raw)
    along = jnp.sum(direction * back, axis=1, keepdims=True)
    return ((back - direction * along) / norm).astype(BF16)


def text_grad_kernel(raw_ref, loss_ref, parts_ref, out_ref, total_ref, raw, grad, sem):
    copies = run([pltpu.make_async_copy(raw_ref, raw, sem.at[0])])
    total = loss_ref[:1, :1]
    for k in range(PEERS):
        total += untag(parts_ref[(k + 1) * PART - MARK : (k + 1) * PART, :].astype(F32)[:1])
    total_ref[0] = (total * (LN2 / (2.0 * SIDE * PEERS)))[0, 0]
    columns = []
    for b in range(WIDTH // 128):
        column = jnp.zeros((PIECE, 128), F32)
        for k in range(PEERS):
            start = k * PART + b * PIECE
            column += parts_ref[start : start + PIECE, :].astype(F32)
        columns.append(column)
    wait(copies)
    grad[...] = project(jnp.concatenate(columns, axis=1), raw[...])
    wait(run([pltpu.make_async_copy(grad, out_ref, sem.at[0])]))


def image_grad_kernel(at_ref, sums_ref, raw_ref, own_ref, below_ref, above_ref, out_ref, loss_ref, raw, own, grad, sem):
    copies = run([
        pltpu.make_async_copy(raw_ref, raw, sem.at[0]), pltpu.make_async_copy(own_ref, own, sem.at[1])
    ])
    twice = lax.rem(at_ref[3] + DEEP // 2, DEEP)
    lane = lax.broadcasted_iota(jnp.int32, (1, 128), 1)
    marks = place_tag(at_ref, sums_ref) + below_ref[PART - MARK :, :].astype(F32)[:1]
    marks += jnp.where(lane // 4 == twice, 0.0, above_ref[PART - MARK :, :].astype(F32)[:1])
    total = jnp.zeros((1, 1), F32)
    for k in range(DEEP):
        total += untag(marks, 4 * k)
    loss_ref[...] = jnp.broadcast_to(total, loss_ref.shape)
    wait(copies)
    came = [
        below_ref[b * PIECE : (b + 1) * PIECE, :].astype(F32) + above_ref[b * PIECE : (b + 1) * PIECE, :].astype(F32)
        for b in range(WIDTH // 128)
    ]
    back = own[...] + jnp.concatenate(came, axis=1)
    grad[...] = project(back, raw[...])
    wait(run([pltpu.make_async_copy(grad, out_ref, sem.at[0])]))


def gather_image(unit):
    plan, arrays = [(0, 0, 0, PIECE)], [unit]
    up, down, half = unit, unit, PIECE // 2
    for by in range(1, DEEP // 2):
        up, down = send(up, "z", 1), send(down, "z", -1)
        plan += [(0, -by, 0, PIECE), (0, by, 0, PIECE)]
        arrays += [up, down]
    plan += [(0, -(DEEP // 2), 0, half), (0, DEEP // 2, half, half)]
    arrays += [send(up[:half], "z", 1), send(down[half:], "z", -1)]
    plan += [(1, *rest) for _, *rest in plan]
    arrays += [send(a, "c", 1) for a in arrays]
    return plan, arrays


def body(image_emb, text_emb, log_scale):
    width = image_emb.shape[1]
    scale = jnp.exp(log_scale)
    me = lax.axis_index("d")
    z, core, x = me % 8, (me // 8) % 2, me // 64
    at = jnp.stack([me % 16, me // 16, core, z, x % 2]).astype(jnp.int32)
    piece = local((PIECE, width), BF16)
    side = local((SIDE, width), BF16)
    outside = array((SIDE, width), BF16)
    raw = pltpu.VMEM((PIECE, width), BF16)
    sems = pltpu.SemaphoreType.DMA

    text_units, image_unit, pairs = call(
        units_kernel, [outside, array((PIECE, width), BF16), local((8, 128), F32)],
        Outside(text_emb), Outside(image_emb), scratch=[raw] * 4 + [sems((2,)), sems((PEERS + 1,))],
    )
    plan, pieces = gather_image(image_unit)
    text = exchange(text_units, XY)


    lines = local((2 * STEPS, TILE), F32)
    image, logits, keep, give = call(
        functools.partial(logits_kernel, plan), [outside, local((SIDE, SIDE), F32), lines, lines],
        at, scale, pairs, text, *map(Outside, pieces),
        scratch=[pltpu.VMEM((SIDE, width), BF16), sems((len(plan),)), sems((2,))],
    )
    spread = call(spread_kernel, local((PEERS * LINES, TILE), F32), at, keep, send(give, "c", 1))
    lines = local((2 * STEPS, TILE), F32)
    keep, give = call(join_kernel, [lines, lines], at, exchange(spread, MIXED))
    recv = send(give, "c", 1)

    half = (SIDE // 2, width)
    weights, turned, other, sums = call(
        weights_kernel,
        [local((SIDE // 2, SIDE), BF16), local((SIDE, SIDE), BF16), local(half, BF16), local((2 * STEPS, 128), F32)],
        at, scale, logits, text, keep, recv,
    )
    swapped = send(other, "c", 1)
    parts = array((PEERS * PART, 128), BF16)
    text_parts, mine = call(
        text_back_kernel, [parts, local(half, F32)], scale, weights, turned, image, text, sums,
        scratch=[pltpu.VMEM(parts.shape, BF16), sems((2,))],
    )
    end = array((FIRST, 128), BF16)
    away = [array((PIECE, width), BF16)] * len(AWAY)
    text_parts, own, up, down, *away = call(
        pieces_kernel, [parts, array((PIECE, width), F32), end, end, *away],
        at, sums, mine, swapped, Outside(text_parts),
        scratch=[
            pltpu.VMEM((PIECE, width), F32),
            pltpu.VMEM((len(AWAY), PIECE, width), BF16),
            pltpu.VMEM((2, FIRST, 128), BF16),
            sems((3 + len(AWAY),)),
        ],
        aliases={4: 0},
    )
    text_back = exchange(text_parts, XY)
    below, above = send(up, "z", 1), send(down, "z", -1)
    whole = local((PART, 128), BF16)
    for k in range(3):
        up, down = call(
            relay_kernel, [whole] * 2, at, sums, Outside(away[k]), Outside(away[k + 3]), below, above,
            scratch=[raw, raw, sems((2,))],
        )
        below, above = send(up, "z", 1), send(down, "z", -1)

    grad = array((PIECE, width), BF16)
    grad_image, part = call(
        image_grad_kernel, [grad, local((8, 128), F32)],
        at, sums, Outside(image_emb), Outside(own), below, above,
        scratch=[raw, pltpu.VMEM((PIECE, width), F32), raw, sems((2,))],
    )
    grad_text, loss = call(
        text_grad_kernel, [grad, pltpu.SMEM((1,), F32)], Outside(text_emb), part, text_back,
        scratch=[raw, raw, sems((1,))],
    )
    return loss, grad_image, grad_text


def solution(mesh):
    flat = Mesh(mesh.devices.reshape(-1), ("d",))
    return jax.shard_map(
        body,
        mesh=flat,
        in_specs=(P("d", None), P("d", None), P()),
        out_specs=(P(), P("d", None), P("d", None)),
        check_vma=False,
    )
```

```python
import functools
import math
import typing

import jax
import jax.numpy as jnp
import numpy as np
from jax import lax
from jax.experimental import pallas as pl
from jax.experimental.pallas import tpu as pltpu
from jax.sharding import Mesh, PartitionSpec as P

LOG2E = math.log2(math.e)
LN2 = math.log(2.0)
EPS = 1e-06
LOW = -1e30
PARAMS = pltpu.CompilerParams(vmem_limit_bytes=24 * 1024 * 1024)
HBM = pl.BlockSpec(memory_space=pl.ANY)
WHOLE = pl.BlockSpec(memory_space=pltpu.VMEM)
SCALAR = pl.BlockSpec(memory_space=pltpu.SMEM)
F32 = jnp.float32
BF16 = jnp.bfloat16

INDEX = np.arange(256).reshape(4, 4, 2, 8)
AXES = {"x": 0, "y": 1, "c": 2, "z": 3}
XY = INDEX.transpose(2, 3, 0, 1).reshape(16, 16).tolist()
MIXED = INDEX[:, :, 0, :].transpose(2, 0, 1).reshape(8, 16).tolist() + (
    INDEX[:, :, 1, :].reshape(2, 2, 4, 8).transpose(0, 2, 1, 3).reshape(8, 16).tolist()
)
PEERS = 16
PIECE = 64
SIDE = PEERS * PIECE
TILE = 256
STEPS = SIDE // TILE
DEEP = 8
LINES = 2 * STEPS
WIDTH = 1280
MARK = 16
PART = PIECE * (WIDTH // 128) + MARK


def shift(axis, by):
    to = np.roll(INDEX, -by, AXES[axis])
    return [(int(a), int(b)) for a, b in zip(INDEX.ravel(), to.ravel())]


def send(x, axis, by):
    return lax.ppermute(x, "d", shift(axis, by))


def exchange(x, groups):
    return lax.all_to_all(x, "d", 0, 0, axis_index_groups=groups, tiled=True)


def array(shape, dtype):
    return pltpu.HBM(shape, dtype)


def local(shape, dtype):
    return pltpu.VMEM(shape, dtype)


def call(kernel, outputs, *operands, scratch=(), aliases={}):
    specs, arrays = [], []
    for x in operands:
        if isinstance(x, Outside):
            specs.append(HBM)
            arrays.append(pltpu.with_memory_space_constraint(x.array, pltpu.HBM))
        elif x.size <= 8:
            specs.append(SCALAR)
            arrays.append(x)
        else:
            specs.append(WHOLE)
            arrays.append(pltpu.with_memory_space_constraint(x, pltpu.VMEM))
    return pl.pallas_call(
        kernel,
        out_shape=outputs,
        in_specs=specs,
        out_specs=jax.tree.map(lambda s: {pltpu.VMEM: WHOLE, pltpu.SMEM: SCALAR}.get(s.memory_space, HBM), outputs),
        scratch_shapes=list(scratch),
        input_output_aliases=aliases,
        compiler_params=PARAMS,
    )(*arrays)


class Outside(typing.NamedTuple):
    array: typing.Any


def run(copies):
    for copy in copies:
        copy.start()
    return copies


def wait(copies):
    for copy in copies:
        copy.wait()


def unit_rows(raw):
    values = raw.astype(F32)
    norm = jnp.sqrt(jnp.sum(values * values, axis=1, keepdims=True) + EPS)
    return values / norm, norm


def units_kernel(
    text_ref, image_ref, text_out, image_out, pairs_ref, text_raw, image_raw, text, image, sem, out_sem
):
    copies = run([
        pltpu.make_async_copy(text_ref, text_raw, sem.at[0]), pltpu.make_async_copy(image_ref, image_raw, sem.at[1])
    ])
    copies[0].wait()
    text[...] = unit_rows(text_raw[...])[0].astype(BF16)
    out = run([
        pltpu.make_async_copy(text, text_out.at[pl.ds(k * PIECE, PIECE), :], out_sem.at[k]) for k in range(PEERS)
    ])
    copies[1].wait()
    image[...] = unit_rows(image_raw[...])[0].astype(BF16)
    out += run([pltpu.make_async_copy(image, image_out, out_sem.at[PEERS])])
    total = jnp.sum(image[...].astype(F32) * text[...].astype(F32), keepdims=True)
    pairs_ref[...] = jnp.broadcast_to(total, pairs_ref.shape)
    wait(out)


def to_lanes(column):
    return jnp.broadcast_to(column, (column.shape[0], 128)).T[:1, :]


def to_rows(lanes):
    return jnp.broadcast_to(lanes, (128, lanes.shape[1])).T[:, :1]


def rows_of(at_ref, by, start, rows):
    first = lax.rem(at_ref[3] + by + DEEP, DEEP) * PIECE + start
    return pl.ds(pl.multiple_of(first, 32), rows)


def near_kernel(plan, at_ref, *refs):
    pieces, (near_out, first_ref, near, sem, out_sem) = refs[: len(plan)], refs[len(plan) :]
    wait(run([
        pltpu.make_async_copy(piece, near.at[rows_of(at_ref, *rest), :], sem.at[k])
        for k, (piece, rest) in enumerate(zip(pieces, plan))
    ]))
    out = run([pltpu.make_async_copy(near, near_out, out_sem.at[0])])
    first_ref[...] = near[:TILE, :]
    wait(out)


def logits_kernel(plan, at_ref, scale_ref, pairs_ref, text_ref, first_ref, near_ref, *refs):
    pieces = refs[: len(plan)]
    far_out, logits_ref, keep_ref, give_ref, second, far, sem, near_sem, out_sem = refs[len(plan) :]
    core = at_ref[2]
    near = run([pltpu.make_async_copy(near_ref.at[pl.ds(TILE, TILE), :], second, near_sem.at[0])])
    copies = run([
        pltpu.make_async_copy(piece, far.at[rows_of(at_ref, *rest), :], sem.at[k])
        for k, (piece, rest) in enumerate(zip(pieces, plan))
    ])
    text = text_ref[...]
    scale = scale_ref[0] * LOG2E
    top = jnp.full((1, SIDE), LOW, F32)
    sums = jnp.zeros((1, SIDE), F32)
    row_lse = []
    for k in range(STEPS):
        tile = slice(k * TILE, (k + 1) * TILE)
        if k == 1:
            wait(near)
        if k == STEPS // 2:
            wait(copies)
            out = run([pltpu.make_async_copy(far, far_out, out_sem.at[0])])
        image = (first_ref, second, far.at[pl.ds(0, TILE), :], far.at[pl.ds(TILE, TILE), :])[k][...]
        logits = scale * lax.dot_general(
            image, text, (((1,), (1,)), ((), ())), preferred_element_type=F32
        )
        logits_ref[tile, :] = logits
        row_top = jnp.max(logits, axis=1, keepdims=True)
        row_sum = jnp.sum(jnp.exp2(logits - row_top), axis=1, keepdims=True)
        row_lse.append(to_lanes(row_top + jnp.log2(row_sum)))
        new = jnp.maximum(top, jnp.max(logits, axis=0, keepdims=True))
        sums = sums * jnp.exp2(top - new) + jnp.sum(jnp.exp2(logits - new), axis=0, keepdims=True)
        top = new
    col_lse = top + jnp.log2(sums)
    first = core == 0
    for k in range(STEPS):
        part = col_lse[:, k * TILE : (k + 1) * TILE]
        keep_ref[k : k + 1, :] = jnp.where(first, part, row_lse[k])
        give_ref[k : k + 1, :] = jnp.where(first, row_lse[(k + STEPS // 2) % STEPS], part)
    pairs = jnp.broadcast_to(pairs_ref[:1, :1] * scale, (STEPS, TILE))
    keep_ref[STEPS:, :] = pairs
    give_ref[STEPS:, :] = pairs
    wait(out)


def spread_kernel(at_ref, keep_ref, recv_ref, out_ref):
    keep, recv = keep_ref[:STEPS, :], recv_ref[:STEPS, :]
    top = jnp.maximum(keep, recv)
    both = top + jnp.log2(jnp.exp2(keep - top) + jnp.exp2(recv - top))
    pairs = keep_ref[STEPS:, :] + recv_ref[STEPS:, :]
    first = at_ref[2] == 0
    block = jnp.concatenate([jnp.where(first, keep, both), jnp.where(first, recv, pairs)], axis=0)
    for k in range(PEERS):
        out_ref[pl.ds(k * LINES, LINES), :] = block


def join_kernel(at_ref, parts_ref, keep_ref, give_ref):
    parts = parts_ref[...].reshape(PEERS, LINES, TILE)
    half = lax.broadcasted_iota(jnp.int32, parts.shape, 0) // DEEP
    first = at_ref[2] == 0
    used = first | (half == at_ref[4])
    pairs = jnp.sum(jnp.where(used, parts, 0.0)[:, STEPS:, :1], axis=0)[:1]
    parts = jnp.where(used, parts, LOW)
    top = jnp.max(parts, axis=0)
    lse = top + jnp.log2(jnp.sum(jnp.exp2(parts - top[None]), axis=0))
    low = jnp.sum(lse[:STEPS], keepdims=True)
    high = jnp.sum(lse[STEPS:], keepdims=True)
    term = jnp.broadcast_to(jnp.where(first, low + high, low - 2.0 * pairs), (STEPS, TILE))
    keep_ref[:STEPS, :] = lse[:STEPS]
    keep_ref[STEPS:, :] = term
    turned = jnp.concatenate([lse[STEPS // 2 : STEPS], lse[: STEPS // 2]], axis=0)
    give_ref[:STEPS, :] = jnp.where(first, lse[STEPS:], turned)
    give_ref[STEPS:, :] = term


def tag(term, rows=PIECE):
    term = jnp.broadcast_to(term, (rows, 128))
    high = term.astype(BF16).astype(F32)
    middle = (term - high).astype(BF16).astype(F32)
    low = (term - high) - middle
    lane = lax.rem(lax.broadcasted_iota(jnp.int32, (rows, 128), 1), 4)
    return jnp.where(lane == 0, high, jnp.where(lane == 1, middle, low)).astype(BF16)


def place_tag(at_ref, sums_ref):
    lane = lax.broadcasted_iota(jnp.int32, (1, 128), 1)
    mark = tag(sums_ref[STEPS : STEPS + 1, :1], 16).astype(F32)[:1]
    return jnp.where(lane // 4 == at_ref[3], mark, 0.0)


def untag(row, lane=0):
    return (row[:, lane : lane + 1] + row[:, lane + 1 : lane + 2]) + row[:, lane + 2 : lane + 3]


def weights_kernel(
    at_ref, scale_ref, logits_ref, text_ref, keep_ref, recv_ref,
    weights_ref, turned_ref, other_ref, sums_ref,
):
    first = at_ref[2] == 0
    keep, recv = keep_ref[:STEPS, :], recv_ref[:STEPS, :]
    cols = jnp.where(first, keep, recv)
    col_lse = jnp.concatenate([cols[k : k + 1] for k in range(STEPS)], axis=1)
    rows = jnp.where(first, recv, keep)
    sums_ref[:STEPS, :] = jnp.where(first, recv_ref[STEPS:, :128], keep_ref[STEPS:, :128])
    sums_ref[STEPS:, :] = jnp.where(first, keep_ref[STEPS:, :128], recv_ref[STEPS:, :128])
    row_at = lax.broadcasted_iota(jnp.int32, (TILE, 1), 0) - at_ref[3] * PIECE
    col_at = lax.broadcasted_iota(jnp.int32, (1, SIDE), 1) - at_ref[1] * PIECE
    col_at = jnp.where((col_at >= 0) & (col_at < PIECE), col_at, -SIDE)
    text = text_ref[...]
    for k in (2, 3, 0, 1):
        tile = slice(k * TILE, (k + 1) * TILE)
        logits = logits_ref[tile, :]
        weights = jnp.exp2(logits - to_rows(rows[k : k + 1])) + jnp.exp2(logits - col_lse)
        if k < STEPS // 2:
            weights -= jnp.where(row_at + k * TILE == col_at, 2.0, 0.0)
        weights = (weights * 0.5).astype(BF16)
        turned_ref[:, tile] = weights.T
        if k < STEPS // 2:
            weights_ref[tile, :] = weights
        else:
            other_ref[(k - 2) * TILE : (k - 1) * TILE, :] = (
                scale_ref[0] * jnp.dot(weights, text, preferred_element_type=F32)
            ).astype(BF16)


def text_back_kernel(scale_ref, weights_ref, turned_ref, near_ref, far_ref, text_ref, sums_ref, out_ref, mine_ref, back, sem):
    near, far = near_ref[...], far_ref[...]
    mark = tag(sums_ref[:1, :1], MARK)
    half = PEERS // 2
    copies = []
    for h in range(2):
        turned = turned_ref[h * half * PIECE : (h + 1) * half * PIECE, :]
        term = jnp.dot(turned[:, : SIDE // 2], near, preferred_element_type=F32)
        term += jnp.dot(turned[:, SIDE // 2 :], far, preferred_element_type=F32)
        term = (scale_ref[0] * term).astype(BF16)
        for p in range(half):
            start = (h * half + p) * PART
            for b in range(WIDTH // 128):
                back[start + b * PIECE : start + (b + 1) * PIECE, :] = (
                    term[p * PIECE : (p + 1) * PIECE, b * 128 : (b + 1) * 128]
                )
            back[start + PART - MARK : start + PART, :] = mark
        span = pl.ds(h * half * PART, half * PART)
        copies += run([pltpu.make_async_copy(back.at[span, :], out_ref.at[span, :], sem.at[h])])
    mine_ref[...] = scale_ref[0] * jnp.dot(weights_ref[...], text_ref[...], preferred_element_type=F32)
    wait(copies)


HALF = PIECE // 2
FIRST = HALF * (WIDTH // 128) + MARK
AWAY = (3, 2, 1, -3, -2, -1)


def pieces_kernel(at_ref, sums_ref, mine_ref, swapped_ref, begun_ref, out_ref, *refs):
    own_out, up_out, down_out, *away_refs, own, parts, ends, sem = refs

    def block(by):
        rows = pl.ds(pl.multiple_of(lax.rem(at_ref[3] + by + DEEP, DEEP) * PIECE, PIECE), PIECE)
        return mine_ref[rows, :] + swapped_ref[rows, :].astype(F32)

    copies = []
    for k, (by, ref) in enumerate(zip(AWAY, away_refs)):
        parts[k] = block(by).astype(BF16)
        copies += run([pltpu.make_async_copy(parts.at[k], ref, sem.at[3 + k])])
    own[...] = block(0)
    copies += run([pltpu.make_async_copy(own, own_out, sem.at[2])])
    across = block(4).astype(BF16)
    mark = jnp.broadcast_to(place_tag(at_ref, sums_ref), (MARK, 128)).astype(BF16)
    for h, out in enumerate((up_out, down_out)):
        for b in range(WIDTH // 128):
            ends[h, b * HALF : (b + 1) * HALF, :] = across[h * HALF : (h + 1) * HALF, b * 128 : (b + 1) * 128]
        ends[h, FIRST - MARK :, :] = mark
        copies += run([pltpu.make_async_copy(ends.at[h], out, sem.at[h])])
    wait(copies)


def relay_kernel(
    at_ref, sums_ref, up_ref, down_ref, below_ref, above_ref, up_out, down_out, up, down, sem
):
    copies = run([pltpu.make_async_copy(up_ref, up, sem.at[0]), pltpu.make_async_copy(down_ref, down, sem.at[1])])
    mark = place_tag(at_ref, sums_ref)
    for k, (copy, ours, theirs, out) in enumerate(
        zip(copies, (up, down), (below_ref, above_ref), (up_out, down_out))
    ):
        size = theirs.shape[0]
        rows = (size - MARK) // (WIDTH // 128)
        marks = theirs[size - MARK :, :].astype(F32)[:1] + mark
        out[PART - MARK :, :] = jnp.broadcast_to(marks, (MARK, 128)).astype(BF16)
        copy.wait()
        for b in range(WIDTH // 128):
            block = ours[:, b * 128 : (b + 1) * 128].astype(F32)
            came = theirs[b * rows : (b + 1) * rows, :].astype(F32)
            if rows < PIECE:
                rest = jnp.zeros_like(came)
                came = jnp.concatenate([came, rest] if k == 0 else [rest, came], axis=0)
            out[b * PIECE : (b + 1) * PIECE, :] = (block + came).astype(BF16)


def project(back, raw):
    direction, norm = unit_rows(raw)
    along = jnp.sum(direction * back, axis=1, keepdims=True)
    return ((back - direction * along) / norm).astype(BF16)


def text_grad_kernel(raw_ref, loss_ref, parts_ref, out_ref, total_ref, raw, grad, sem):
    copies = run([pltpu.make_async_copy(raw_ref, raw, sem.at[0])])
    total = loss_ref[:1, :1]
    for k in range(PEERS):
        total += untag(parts_ref[(k + 1) * PART - MARK : (k + 1) * PART, :].astype(F32)[:1])
    total_ref[0] = (total * (LN2 / (2.0 * SIDE * PEERS)))[0, 0]
    columns = []
    for b in range(WIDTH // 128):
        column = jnp.zeros((PIECE, 128), F32)
        for k in range(PEERS):
            start = k * PART + b * PIECE
            column += parts_ref[start : start + PIECE, :].astype(F32)
        columns.append(column)
    wait(copies)
    grad[...] = project(jnp.concatenate(columns, axis=1), raw[...])
    wait(run([pltpu.make_async_copy(grad, out_ref, sem.at[0])]))


def image_grad_kernel(at_ref, sums_ref, raw_ref, own_ref, below_ref, above_ref, out_ref, loss_ref, raw, own, grad, sem):
    copies = run([
        pltpu.make_async_copy(raw_ref, raw, sem.at[0]), pltpu.make_async_copy(own_ref, own, sem.at[1])
    ])
    twice = lax.rem(at_ref[3] + DEEP // 2, DEEP)
    lane = lax.broadcasted_iota(jnp.int32, (1, 128), 1)
    marks = place_tag(at_ref, sums_ref) + below_ref[PART - MARK :, :].astype(F32)[:1]
    marks += jnp.where(lane // 4 == twice, 0.0, above_ref[PART - MARK :, :].astype(F32)[:1])
    total = jnp.zeros((1, 1), F32)
    for k in range(DEEP):
        total += untag(marks, 4 * k)
    loss_ref[...] = jnp.broadcast_to(total, loss_ref.shape)
    wait(copies)
    came = [
        below_ref[b * PIECE : (b + 1) * PIECE, :].astype(F32) + above_ref[b * PIECE : (b + 1) * PIECE, :].astype(F32)
        for b in range(WIDTH // 128)
    ]
    back = own[...] + jnp.concatenate(came, axis=1)
    grad[...] = project(back, raw[...])
    wait(run([pltpu.make_async_copy(grad, out_ref, sem.at[0])]))


def gather_image(unit):
    plan, arrays = [(0, 0, PIECE)], [unit]
    up, down, half = unit, unit, PIECE // 2
    for by in range(1, DEEP // 2):
        up, down = send(up, "z", 1), send(down, "z", -1)
        plan += [(-by, 0, PIECE), (by, 0, PIECE)]
        arrays += [up, down]
    plan += [(-(DEEP // 2), 0, half), (DEEP // 2, half, half)]
    arrays += [send(up[:half], "z", 1), send(down[half:], "z", -1)]
    arrays += [send(a, "c", 1) for a in arrays]
    return plan, arrays


def body(image_emb, text_emb, log_scale):
    width = image_emb.shape[1]
    scale = jnp.exp(log_scale)
    me = lax.axis_index("d")
    z, core, x = me % 8, (me // 8) % 2, me // 64
    at = jnp.stack([me % 16, me // 16, core, z, x % 2]).astype(jnp.int32)
    piece = local((PIECE, width), BF16)
    side = local((SIDE, width), BF16)
    outside = array((SIDE, width), BF16)
    raw = pltpu.VMEM((PIECE, width), BF16)
    sems = pltpu.SemaphoreType.DMA

    text_units, image_unit, pairs = call(
        units_kernel, [outside, array((PIECE, width), BF16), local((8, 128), F32)],
        Outside(text_emb), Outside(image_emb), scratch=[raw] * 4 + [sems((2,)), sems((PEERS + 1,))],
    )
    plan, pieces = gather_image(image_unit)
    text = exchange(text_units, XY)


    half = (SIDE // 2, width)
    side = pltpu.VMEM(half, BF16)
    near, first = call(
        functools.partial(near_kernel, plan), [array(half, BF16), local((TILE, width), BF16)],
        at, *map(Outside, pieces[: len(plan)]), scratch=[side, sems((len(plan),)), sems((1,))],
    )
    lines = local((2 * STEPS, TILE), F32)
    far, logits, keep, give = call(
        functools.partial(logits_kernel, plan), [array(half, BF16), local((SIDE, SIDE), F32), lines, lines],
        at, scale, pairs, text, first, Outside(near), *map(Outside, pieces[len(plan) :]),
        scratch=[pltpu.VMEM((TILE, width), BF16), side, sems((len(plan),)), sems((1,)), sems((1,))],
    )
    spread = call(spread_kernel, local((PEERS * LINES, TILE), F32), at, keep, send(give, "c", 1))
    lines = local((2 * STEPS, TILE), F32)
    keep, give = call(join_kernel, [lines, lines], at, exchange(spread, MIXED))
    recv = send(give, "c", 1)

    weights, turned, other, sums = call(
        weights_kernel,
        [local((SIDE // 2, SIDE), BF16), local((SIDE, SIDE), BF16), local(half, BF16), local((2 * STEPS, 128), F32)],
        at, scale, logits, text, keep, recv,
    )
    swapped = send(other, "c", 1)
    parts = array((PEERS * PART, 128), BF16)
    text_parts, mine = call(
        text_back_kernel, [parts, local(half, F32)], scale, weights, turned, near, far, text, sums,
        scratch=[pltpu.VMEM(parts.shape, BF16), sems((2,))],
    )
    end = array((FIRST, 128), BF16)
    away = [array((PIECE, width), BF16)] * len(AWAY)
    text_parts, own, up, down, *away = call(
        pieces_kernel, [parts, array((PIECE, width), F32), end, end, *away],
        at, sums, mine, swapped, Outside(text_parts),
        scratch=[
            pltpu.VMEM((PIECE, width), F32),
            pltpu.VMEM((len(AWAY), PIECE, width), BF16),
            pltpu.VMEM((2, FIRST, 128), BF16),
            sems((3 + len(AWAY),)),
        ],
        aliases={4: 0},
    )
    text_back = exchange(text_parts, XY)
    below, above = send(up, "z", 1), send(down, "z", -1)
    whole = local((PART, 128), BF16)
    for k in range(3):
        up, down = call(
            relay_kernel, [whole] * 2, at, sums, Outside(away[k]), Outside(away[k + 3]), below, above,
            scratch=[raw, raw, sems((2,))],
        )
        below, above = send(up, "z", 1), send(down, "z", -1)

    grad = array((PIECE, width), BF16)
    grad_image, part = call(
        image_grad_kernel, [grad, local((8, 128), F32)],
        at, sums, Outside(image_emb), Outside(own), below, above,
        scratch=[raw, pltpu.VMEM((PIECE, width), F32), raw, sems((2,))],
    )
    grad_text, loss = call(
        text_grad_kernel, [grad, pltpu.SMEM((1,), F32)], Outside(text_emb), part, text_back,
        scratch=[raw, raw, sems((1,))],
    )
    return loss, grad_image, grad_text


def solution(mesh):
    flat = Mesh(mesh.devices.reshape(-1), ("d",))
    return jax.shard_map(
        body,
        mesh=flat,
        in_specs=(P("d", None), P("d", None), P()),
        out_specs=(P(), P("d", None), P("d", None)),
        check_vma=False,
    )
```
